32 devices in a mesh: frame: 8 (over z, x), strip: 4 (over y, core).
Axes of the slice: x: 2, y: 2, z: 4, core: 2. Of those that a mesh axis runs over, the one named last changes fastest.
Arguments:
- movie: bfloat16 [64, 256, 2048], P('frame', 'strip'), may hold values from -17 to 22, as said below
Outputs:
- lag_maps: float32 [25, 256, 2048], P(None, 'strip', 'frame')
The draws below stay inside these ranges and needn't reach their ends.
Inputs may be any that keep to these rules, and one draw needn't show every extreme that they name: Frames of a camera movie.
All inputs are finite; a program needn't handle non-finite values.
Results may differ from the reference program's by a relative error of at most 0.0004.
Values may be sent and summed in bfloat16 or wider, within the bound.
No kernel may reach another device: no remote copies, remote signals or barrier semaphores. Data moves between devices by JAX's collectives and lax.ppermute only.
A program may use at most 64 MiB of HBM per device.

```python
import math
import jax
import jax.numpy as jnp
from jax import lax

FR_DEV = 8
WIDTH = 2048
LAGS = 25
FRAMES = 64
HEIGHT = 256
N_FRAME = 8


def draw_movie(key, part):
    key_offset = jax.random.fold_in(key, 11)
    key_scale = jax.random.fold_in(key, 12)
    key_noise = jax.random.fold_in(key, 13)
    offset = jnp.exp(jax.random.uniform(key_offset, (HEIGHT, WIDTH), jnp.float32, 0.0, math.log(4.0)))
    pixel_scale = jnp.exp(jax.random.uniform(key_scale, (HEIGHT, WIDTH), jnp.float32, -math.log(2.0), math.log(2.0)))
    noise_field = jnp.clip(jax.random.normal(key_noise, (FRAMES, HEIGHT, WIDTH), jnp.float32), -4.0, 4.0)
    blurred = noise_field + 0.6 * jnp.roll(noise_field, 1, axis=1) + 0.6 * jnp.roll(noise_field, 1, axis=2)
    return (offset + pixel_scale * blurred).astype(jnp.bfloat16)


def setup_inputs(seed: int = 0) -> dict:
    key_of = jax.random.split(jax.random.key(seed), 2)
    movie = draw_movie(jax.random.fold_in(key_of[1], 71), 0)
    return {"movie": movie}


def reference(movie):
    frame_blocks = movie.reshape(N_FRAME, FR_DEV, HEIGHT, WIDTH)

    def add_sum(running, movie_block):
        return running + jnp.sum(movie_block.astype(jnp.float32), axis=0), None

    running, _ = lax.scan(add_sum, jnp.zeros((HEIGHT, WIDTH), jnp.float32), frame_blocks)
    pixel_mean = running / FRAMES

    def add_lags(lag_total, movie_block):
        fluctuation = movie_block.astype(jnp.float32) - pixel_mean
        padded = jnp.pad(fluctuation, ((0, 0), (2, 2), (2, 2)))
        centre = padded[:, 2:2 + HEIGHT, 2:2 + WIDTH]
        products = []
        for row_lag in range(-2, 3):
            for col_lag in range(-2, 3):
                shifted = padded[:, 2 + row_lag:2 + row_lag + HEIGHT, 2 + col_lag:2 + col_lag + WIDTH]
                products.append(jnp.sum(centre * shifted, axis=0))
        return lag_total + jnp.stack(products), None

    lag_total, _ = lax.scan(add_lags, jnp.zeros((LAGS, HEIGHT, WIDTH), jnp.float32), frame_blocks)
    return lag_total / FRAMES
```

```python
import jax
import jax.numpy as jnp
from jax import lax
from jax.experimental import pallas as pl
from jax.experimental.pallas import tpu as pltpu
from jax.sharding import PartitionSpec as P

REACH = 2
LANES = 128
GROUP = 8
PAIR = 2 * GROUP
LAG_LIST = tuple(
    (a, b)
    for a in range(REACH + 1)
    for b in range(-REACH, REACH + 1)
    if a > 0 or b >= 0
)
VMEM = 56 * 1024 * 1024


def shifted(ring, index, offset):
    tile = ring[index]
    if offset == 0:
        return tile
    lane = lax.broadcasted_iota(jnp.int32, tile.shape, tile.ndim - 1)
    if offset > 0:
        other = ring[(index + 1) % len(ring)]
        mixed = jnp.where(lane < offset, other, tile)
    else:
        other = ring[index - 1]
        mixed = jnp.where(lane >= LANES + offset, other, tile)
    return pltpu.roll(mixed, (-offset) % LANES, 1)


def both_rows(ref, index, row, stride):
    return jnp.concatenate(
        [ref[index, pl.ds(row + j, GROUP, stride=stride), :] for j in range(2)], axis=0
    )


def write_packed(ref, places, rows, outs):
    lane = lax.broadcasted_iota(jnp.int32, (PAIR, LANES), 1)
    zero = jnp.zeros((PAIR, LANES), jnp.float32)

    def pair(q, edges):
        result = []
        for (own, left, right), out, edge in zip(places, outs, edges):
            for t, place in enumerate(own):
                start = pl.multiple_of((t * rows + 2 * q) * GROUP, PAIR)
                both = both_rows(ref, place, 2 * q, rows)
                out[pl.ds(start, PAIR), :] = both.astype(jnp.bfloat16)
            sides = jnp.where(
                lane >= LANES - REACH,
                both_rows(ref, left, 2 * q, rows),
                both_rows(ref, right, 2 * q, rows),
            )
            first = 2 * REACH * q
            placed = pltpu.roll(sides, first + REACH, 1)
            inside = (lane >= first) & (lane < first + 2 * REACH)
            result.append(jnp.where(inside, placed, edge))
        return tuple(result)

    edges = lax.fori_loop(0, rows // 2, pair, (zero,) * len(outs), unroll=4)
    for (own, _, _), out, edge in zip(places, outs, edges):
        out[len(own) * rows * GROUP :, :] = edge.astype(jnp.bfloat16)


def pack_one_kernel(tiles, block_ref, main_ref, left_ref, right_ref, out_ref, values):
    frames, rows, _ = main_ref.shape
    block, blocks = block_ref[0], block_ref[1]
    flat = (frames * rows, LANES)
    for t in range(tiles):
        part = main_ref[:, :, t * LANES : (t + 1) * LANES]
        values[t] = part.astype(jnp.float32).reshape(flat)
    left = left_ref[...].astype(jnp.float32).reshape(flat)
    right = right_ref[...].astype(jnp.float32).reshape(flat)
    values[tiles] = jnp.where(block > 0, left, 0.0)
    values[tiles + 1] = jnp.where(block < blocks - 1, right, 0.0)
    places = [(list(range(tiles)), tiles, tiles + 1)]
    write_packed(values, places, rows, [out_ref])


def packed_length(rows, tiles):
    return tiles * rows * GROUP + PAIR


def pack_one(movie, block, blocks):
    frames, rows, width = movie.shape
    columns = width // blocks
    tiles = columns // LANES
    last = width // LANES - 1
    length = packed_length(rows, tiles)
    return pl.pallas_call(
        lambda *refs: pack_one_kernel(tiles, *refs),
        out_shape=jax.ShapeDtypeStruct((length, LANES), jnp.bfloat16),
        grid_spec=pltpu.PrefetchScalarGridSpec(
            num_scalar_prefetch=1,
            grid=(1,),
            in_specs=[
                pl.BlockSpec((frames, rows, columns), lambda i, s: (0, 0, s[0])),
                pl.BlockSpec(
                    (frames, rows, LANES),
                    lambda i, s: (0, 0, jnp.maximum(s[0] * tiles - 1, 0)),
                ),
                pl.BlockSpec(
                    (frames, rows, LANES),
                    lambda i, s: (0, 0, jnp.minimum(s[0] * tiles + tiles, last)),
                ),
            ],
            out_specs=pl.BlockSpec((length, LANES), lambda i, s: (0, 0)),
            scratch_shapes=[pltpu.VMEM((tiles + 2, frames * rows, LANES), jnp.float32)],
        ),
        compiler_params=pltpu.CompilerParams(vmem_limit_bytes=VMEM),
        name="pack_one",
    )(jnp.stack([block, jnp.int32(blocks)]), movie, movie, movie)


def pack_kernel(tiles, me_ref, movie_ref, *refs):
    outs, values = refs[:-1], refs[-1]
    frames, rows, width = movie_ref.shape
    count = width // LANES
    blocks = count // tiles
    flat = (frames * rows, LANES)
    zero = jnp.zeros(flat, jnp.float32)
    values[0] = zero
    values[count + 1] = zero
    for t in range(count):
        part = movie_ref[:, :, t * LANES : (t + 1) * LANES]
        values[t + 1] = part.astype(jnp.float32).reshape(flat)
    places = []
    for k in range(blocks):
        if outs[k] is None:
            continue
        first = 1 + (me_ref[0] ^ k) * tiles
        places.append(([first + t for t in range(tiles)], first - 1, first + tiles))
    write_packed(values, places, rows, [out for out in outs if out is not None])


def pack_rest(movie, me, blocks, skip):
    frames, rows, width = movie.shape
    tiles = width // blocks // LANES
    length = packed_length(rows, tiles)
    whole = pl.BlockSpec(memory_space=pltpu.VMEM)
    kept = [k for k in range(blocks) if k != skip]

    def kernel(me_ref, movie_ref, *refs):
        outs = list(refs[:-1])
        outs.insert(skip, None)
        pack_kernel(tiles, me_ref, movie_ref, *outs, refs[-1])

    results = pl.pallas_call(
        kernel,
        out_shape=[jax.ShapeDtypeStruct((length, LANES), jnp.bfloat16)] * len(kept),
        in_specs=[pl.BlockSpec(memory_space=pltpu.SMEM), whole],
        out_specs=[whole] * len(kept),
        scratch_shapes=[
            pltpu.VMEM((width // LANES + 2, frames * rows, LANES), jnp.float32)
        ],
        compiler_params=pltpu.CompilerParams(vmem_limit_bytes=VMEM),
        name="pack_rest",
    )(me[None], movie)
    return dict(zip(kept, results))


def lag_kernel(tiles, rows, frames, sources, has_prior, last, *refs):
    refs = list(refs)
    blocks = [refs[3 * i : 3 * i + 3] for i in range(sources + 1)]
    refs = refs[3 * sources + 3 :]
    prior = None
    if has_prior:
        prior, prior_sum = refs[:2]
        refs = refs[2:]
    if last:
        out, rings, shifts, parts, maps, sums, sum_shifts, cov = refs
    else:
        maps, sums, rings, shifts, parts = refs
    ring = tiles + 1
    span = (rows + 2 * REACH) * GROUP

    def unfold(edge, index):
        return pltpu.roll(edge, (-2 * REACH * index - REACH) % LANES, 1)

    def place(i, t, start, value):
        if i == 0:
            value = jnp.concatenate(
                [
                    jnp.broadcast_to(value[j * GROUP : j * GROUP + 1], (GROUP, LANES))
                    for j in range(2)
                ],
                axis=0,
            )
        rings[i, t, pl.ds(start, PAIR), :] = value.astype(jnp.bfloat16)

    main = tiles * rows * GROUP
    for i, (body, above, below) in enumerate(blocks):
        for ref, start, index in ((above, 0, rows // 2 - 1), (below, span - PAIR, 0)):
            for t in range(tiles):
                value = ref[t * PAIR : (t + 1) * PAIR, :].astype(jnp.float32)
                place(i, t, start, value)
            edge = ref[tiles * PAIR :, :].astype(jnp.float32)
            place(i, tiles, start, unfold(edge, index))
        if i > 0:
            for t in range(tiles):
                part = body[t * rows * GROUP : (t + 1) * rows * GROUP, :]
                rings[i, t, PAIR : span - PAIR, :] = part

    tails = [b[0][main:, :].astype(jnp.float32) for b in blocks]

    def fill(q, carry):
        start = pl.multiple_of((q + 1) * PAIR, PAIR)
        shift = lax.rem(2 * LANES - 2 * REACH * q - REACH, LANES)
        for i, (body, _, _) in enumerate(blocks):
            place(i, tiles, start, pltpu.roll(tails[i], shift, 1))
            if i == 0:
                for t in range(tiles):
                    at = pl.multiple_of(t * rows * GROUP + q * PAIR, PAIR)
                    place(i, t, start, body[pl.ds(at, PAIR), :].astype(jnp.float32))
        return carry

    lax.fori_loop(0, rows // 2, fill, 0, unroll=4)

    source = lax.broadcasted_iota(jnp.int32, (2 * LANES, LANES), 0)
    target = lax.broadcasted_iota(jnp.int32, (2 * LANES, LANES), 1)
    moves = jnp.concatenate(
        [jnp.where(source == target + b, 1.0, 0.0) for b in range(1, REACH + 1)], axis=1
    ).astype(jnp.bfloat16)
    size = (rows + 2 * REACH) * GROUP // (2 if sources < 3 else 17)
    if size % PAIR or span % size:
        size = PAIR

    def spread(c, carry):
        at = pl.ds(pl.multiple_of(c * size, PAIR), size)
        raw = [[rings[i, t, at, :] for t in range(ring)] for i in range(sources + 1)]
        wide = jnp.concatenate(
            [
                jnp.concatenate([r[t], r[(t + 1) % ring]], axis=1)
                for r in raw
                for t in range(ring)
            ],
            axis=0,
        )
        moved = jnp.dot(wide, moves, preferred_element_type=jnp.float32)

        def version(i, t, b):
            if b == 0:
                return raw[i][t].astype(jnp.float32)
            first = (i * ring + t) * size
            return moved[first : first + size, (b - 1) * LANES : b * LANES]

        for t in range(ring):
            for b in range(REACH + 1):
                pivot = version(0, t, b)
                for i in range(1, sources + 1):
                    shifts[b, i - 1, t, at, :] = version(i, t, b) - pivot
        return carry

    lax.fori_loop(0, span // size, spread, 0)

    def products(t, slot, lags):
        totals = [[None] * (len(lags) + 1) for _ in range(2)]
        for i in range(sources):
            cache = {}

            def value(step, offset):
                if (step, offset) not in cache:
                    start = pl.multiple_of((slot + step) * GROUP, GROUP)
                    cache[step, offset] = shifts[offset, i, t, pl.ds(start, GROUP), :]
                return cache[step, offset]

            for j in range(2):
                for k, (a, b) in enumerate(lags):
                    term = value(j, max(-b, 0)) * value(j + a, max(b, 0))
                    totals[j][k] = term if i == 0 else totals[j][k] + term
                term = value(j, 0)
                totals[j][-1] = term if i == 0 else totals[j][-1] + term
        return totals

    def folded(k, first):
        terms = [
            parts[k, pl.ds(first + u, GROUP, stride=GROUP), :] for u in range(GROUP)
        ]
        while len(terms) > 1:
            terms = [x + y for x, y in zip(terms[::2], terms[1::2])]
        return terms[0]

    count = len(LAG_LIST)
    lead = GROUP - REACH
    for k in range(count + 1):
        parts[k, : lead * GROUP, :] = jnp.zeros((lead * GROUP, LANES), jnp.float32)
    for t in range(ring):
        wanted = [k for k, (a, b) in enumerate(LAG_LIST) if t < tiles or b != 0]
        lags = [LAG_LIST[k] for k in wanted]

        def pair(q, carry):
            totals = products(t, 2 * q, lags)
            for j in range(2):
                at = pl.ds(pl.multiple_of((lead + 2 * q + j) * GROUP, GROUP), GROUP)
                for n, k in enumerate(wanted + [count]):
                    parts[k, at, :] = totals[j][n]
            return carry

        lax.fori_loop(0, rows // 2 + 1, pair, 0)

        def reduce(g, carry):
            at = pl.ds(pl.multiple_of(g * GROUP, GROUP), GROUP)
            for k in wanted:
                value = folded(k, g * GROUP * GROUP)
                if has_prior:
                    value = value + prior[k, t, at, :]
                maps[k, t, at, :] = value
            value = folded(count, g * GROUP * GROUP)
            if has_prior:
                value = value + prior_sum[t, at, :]
            sums[t, at, :] = value
            return carry

        lax.fori_loop(0, rows // GROUP + 1, reduce, 0)
        for j in range(GROUP):
            start = (rows + min(REACH + j, 2 * REACH - 1)) * GROUP
            v = shifts[0, 0, t, start : start + GROUP, :]
            for i in range(1, sources):
                v = v + shifts[0, i, t, start : start + GROUP, :]
            parts[count, (rows + GROUP + j) * GROUP : (rows + GROUP + j + 1) * GROUP] = v
        value = folded(count, (rows + GROUP) * GROUP)
        if has_prior:
            value = value + prior_sum[t, rows + GROUP :, :]
        sums[t, rows + GROUP :, :] = value

    if last:
        finish(tiles, rows, frames, maps, sums, out, sum_shifts, cov)


def finish(tiles, rows, frames, maps, sums, out, sum_shifts, cov):
    ring = tiles + 1
    scale = 1.0 / frames
    for g in range((rows + 2 * GROUP) // GROUP):
        at = slice(g * GROUP, (g + 1) * GROUP)
        row_ring = [sums[t, at, :] for t in range(ring)]
        for t in range(ring):
            for b in range(REACH + 1):
                sum_shifts[b, t, at, :] = shifted(row_ring, t, b)

    def centred(g, carry):
        start = pl.multiple_of(g * GROUP, GROUP)
        at = pl.ds(start, GROUP)
        for t in range(ring):
            here = [sum_shifts[b, t, at, :] * scale for b in range(REACH + 1)]
            for k, (a, b) in enumerate(LAG_LIST):
                if t == tiles and b == 0:
                    continue
                other = sum_shifts[max(b, 0), t, pl.ds(start + a, GROUP), :]
                mean = here[max(-b, 0)]
                cov[k, t, at, :] = (maps[k, t, at, :] - mean * other) * scale
        return carry

    lax.fori_loop(0, rows // GROUP + 1, centred, 0)

    def write(g, carry):
        start = pl.multiple_of(g * GROUP, GROUP)
        here = pl.ds(start, GROUP)
        for k, (a, b) in enumerate(LAG_LIST):
            index = (2 * REACH + 1) * (a + REACH) + b + REACH
            mirror = (2 * REACH + 1) ** 2 - 1 - index
            for n, first, offset in (
                (index, start + GROUP, min(b, 0)),
                (mirror, start + GROUP - a, min(-b, 0)),
            ):
                row_ring = [
                    cov[k, t, pl.ds(first, GROUP), :] if t < tiles or offset else None
                    for t in range(ring)
                ]
                for t in range(tiles):
                    lanes = slice(t * LANES, (t + 1) * LANES)
                    out[n, here, lanes] = shifted(row_ring, t, offset)
                if index == mirror:
                    break
        return carry

    lax.fori_loop(0, rows // GROUP, write, 0)


def lag_sums(blocks, rows, tiles, frames, prior=None, last=False):
    sources = len(blocks) - 1
    ring = tiles + 1
    span = (rows + 2 * REACH) * GROUP
    operands = [a for block in blocks for a in block] + list(prior or ())
    whole = pl.BlockSpec(memory_space=pltpu.VMEM)
    map_shape = (len(LAG_LIST), ring, rows + GROUP, LANES)
    sum_shape = (ring, rows + 2 * GROUP, LANES)
    scratch = [
        pltpu.VMEM((sources + 1, ring, span, LANES), jnp.bfloat16),
        pltpu.VMEM((REACH + 1, sources, ring, span, LANES), jnp.float32),
        pltpu.VMEM((len(LAG_LIST) + 1, (rows + 2 * GROUP) * GROUP, LANES), jnp.float32),
    ]
    if last:
        out_shape = jax.ShapeDtypeStruct(
            ((2 * REACH + 1) ** 2, rows, tiles * LANES), jnp.float32
        )
        out_specs = whole
        scratch += [
            pltpu.VMEM(map_shape, jnp.float32),
            pltpu.VMEM(sum_shape, jnp.float32),
            pltpu.VMEM((REACH + 1,) + sum_shape, jnp.float32),
            pltpu.VMEM(map_shape, jnp.float32),
        ]
    else:
        out_shape = (
            jax.ShapeDtypeStruct(map_shape, jnp.float32),
            jax.ShapeDtypeStruct(sum_shape, jnp.float32),
        )
        out_specs = (whole, whole)
    return pl.pallas_call(
        lambda *refs: lag_kernel(
            tiles, rows, frames, sources, prior is not None, last, *refs
        ),
        out_shape=out_shape,
        in_specs=[whole] * len(operands),
        out_specs=out_specs,
        scratch_shapes=scratch,
        compiler_params=pltpu.CompilerParams(vmem_limit_bytes=VMEM),
        name="lag_maps" if last else "lag_sums",
    )(*operands)


def edge_blocks(packed, rows, tiles):
    size = rows * GROUP
    tail = packed[tiles * size :]
    first = [packed[t * size : t * size + PAIR] for t in range(tiles)]
    last = [packed[(t + 1) * size - PAIR : (t + 1) * size] for t in range(tiles)]
    return jnp.concatenate(first + [tail]), jnp.concatenate(last + [tail])


def exchange_rows(blocks, rows, tiles):
    strips = lax.axis_size("strip")
    up = [(i, i + 1) for i in range(strips - 1)]
    down = [(j, i) for i, j in up]
    pairs = [edge_blocks(b, rows, tiles) for b in blocks]
    above = lax.ppermute(jnp.stack([last for _, last in pairs]), "strip", up)
    below = lax.ppermute(jnp.stack([first for first, _ in pairs]), "strip", down)
    return [(above[i], below[i]) for i in range(len(blocks))]


def body(movie):
    frames_here, rows, width = movie.shape
    peers = lax.axis_size("frame")
    tiles = width // peers // LANES
    me = lax.axis_index("frame")
    frames = frames_here * peers
    half = peers // 2
    far = list(range(half, peers))
    near = list(range(1, half))
    packed = pack_rest(movie, me, peers, far[0])
    packed[far[0]] = pack_one(movie, me ^ far[0], peers)
    steps = far[:1] + near + far[1:]
    moved = {0: packed[0]}
    for k in steps:
        moved[k] = lax.ppermute(packed[k], "frame", [(i, i ^ k) for i in range(peers)])
    every = [0] + steps
    halos = exchange_rows([moved[k] for k in every], rows, tiles)
    blocks = [(moved[k],) + halo for k, halo in zip(every, halos)]
    half = len(blocks) // 2
    prior = lag_sums(blocks[:1] + blocks[:half], rows, tiles, frames)
    return lag_sums(blocks[:1] + blocks[half:], rows, tiles, frames, prior, True)


def solution(mesh):
    return jax.shard_map(
        body,
        mesh=mesh,
        in_specs=(P("frame", "strip", None),),
        out_specs=P(None, "strip", "frame"),
        check_vma=False,
    )
```

```python
import math

import jax
import jax.numpy as jnp
from jax import lax
from jax.experimental import pallas as pl
from jax.experimental.pallas import tpu as pltpu
from jax.sharding import PartitionSpec as P

REACH = 2
LANES = 128
GROUP = 8
FOLD = LANES // (2 * REACH)
PAD = 2 * REACH
PAIR = 2 * GROUP
LAG_LIST = tuple(
    (a, b)
    for a in range(REACH + 1)
    for b in range(-REACH, REACH + 1)
    if a > 0 or b >= 0
)
def cost(micros):
    work = int(micros * 1e9 * 0.3)
    return pl.CostEstimate(flops=work, bytes_accessed=work // 300, transcendentals=0)


VMEM = 56 * 1024 * 1024


def shifted(ring, index, offset):
    tile = ring[index]
    if offset == 0:
        return tile
    lane = lax.broadcasted_iota(jnp.int32, tile.shape, tile.ndim - 1)
    if offset > 0:
        other = ring[(index + 1) % len(ring)]
        mixed = jnp.where(lane < offset, other, tile)
    else:
        other = ring[index - 1]
        mixed = jnp.where(lane >= LANES + offset, other, tile)
    return pltpu.roll(mixed, (-offset) % LANES, 1)


def folded_pairs(pairs):
    return -(-pairs // FOLD)


def both_rows(ref, index, row, stride):
    return jnp.concatenate(
        [ref[index, pl.ds(row + j, GROUP, stride=stride), :] for j in range(2)], axis=0
    )


def lay_out(ref, place, value, above=None, below=None):
    frames, rows, _ = value.shape
    for f in range(frames):
        start = f * (rows + PAD)
        ref[place, start + REACH : start + REACH + rows, :] = value[f].astype(jnp.float32)
        if above is not None:
            ref[place, start : start + REACH, :] = above[f].astype(jnp.float32)
            end = start + REACH + rows
            ref[place, end : end + REACH, :] = below[f].astype(jnp.float32)


def edge_sides(ref, left, right, row, stride):
    lane = lax.broadcasted_iota(jnp.int32, (PAIR, LANES), 1)
    return jnp.where(
        lane >= LANES - REACH,
        both_rows(ref, left, row, stride),
        both_rows(ref, right, row, stride),
    )


def folded_in(edge, sides, index):
    lane = lax.broadcasted_iota(jnp.int32, (PAIR, LANES), 1)
    first = 2 * REACH * index
    placed = pltpu.roll(sides, first + REACH, 1)
    return jnp.where((lane >= first) & (lane < first + 2 * REACH), placed, edge)


def write_packed(ref, places, rows, offset, outs):
    stride = rows + PAD
    pairs = outs_pairs = rows // 2 + (2 if offset == 0 else 0)
    span = pairs * PAIR
    zero = jnp.zeros((PAIR, LANES), jnp.float32)
    for part in range(folded_pairs(pairs)):

        def pair(q, edges, part=part):
            row = offset + 2 * q
            result = []
            for (own, left, right), out, edge in zip(places, outs, edges):
                for t, place in enumerate(own):
                    start = pl.multiple_of(t * span + q * PAIR, PAIR)
                    both = both_rows(ref, place, row, stride)
                    out[pl.ds(start, PAIR), :] = both.astype(jnp.bfloat16)
                sides = edge_sides(ref, left, right, row, stride)
                result.append(folded_in(edge, sides, q - part * FOLD))
            return tuple(result)

        first, last = part * FOLD, min((part + 1) * FOLD, outs_pairs)
        unroll = 4 if (last - first) % 4 == 0 else 1
        edges = lax.fori_loop(first, last, pair, (zero,) * len(outs), unroll=unroll)
        for (own, _, _), out, edge in zip(places, outs, edges):
            start = len(own) * span + part * PAIR
            out[start : start + PAIR, :] = edge.astype(jnp.bfloat16)


def pack_one_kernel(tiles, block_ref, main_ref, left_ref, right_ref, out_ref, values):
    rows = main_ref.shape[1]
    block, blocks = block_ref[0], block_ref[1]
    for t in range(tiles):
        lay_out(values, t, main_ref[:, :, t * LANES : (t + 1) * LANES])
    lay_out(values, tiles, left_ref[...])
    lay_out(values, tiles + 1, right_ref[...])

    @pl.when(block == 0)
    def _():
        values[tiles] = jnp.zeros(values.shape[1:], jnp.float32)

    @pl.when(block == blocks - 1)
    def _():
        values[tiles + 1] = jnp.zeros(values.shape[1:], jnp.float32)

    places = [(list(range(tiles)), tiles, tiles + 1)]
    write_packed(values, places, rows, REACH, [out_ref])


def packed_length(rows, tiles):
    return tiles * rows * GROUP + folded_pairs(rows // 2) * PAIR


def pack_one(movie, block, blocks):
    frames, rows, width = movie.shape
    columns = width // blocks
    tiles = columns // LANES
    last = width // LANES - 1
    length = packed_length(rows, tiles)
    return pl.pallas_call(
        lambda *refs: pack_one_kernel(tiles, *refs),
        out_shape=jax.ShapeDtypeStruct((length, LANES), jnp.bfloat16),
        grid_spec=pltpu.PrefetchScalarGridSpec(
            num_scalar_prefetch=1,
            grid=(1,),
            in_specs=[
                pl.BlockSpec((frames, rows, columns), lambda i, s: (0, 0, s[0])),
                pl.BlockSpec(
                    (frames, rows, LANES),
                    lambda i, s: (0, 0, jnp.maximum(s[0] * tiles - 1, 0)),
                ),
                pl.BlockSpec(
                    (frames, rows, LANES),
                    lambda i, s: (0, 0, jnp.minimum(s[0] * tiles + tiles, last)),
                ),
            ],
            out_specs=pl.BlockSpec((length, LANES), lambda i, s: (0, 0)),
            scratch_shapes=[
                pltpu.VMEM((tiles + 2, frames * (rows + PAD), LANES), jnp.float32)
            ],
        ),
        compiler_params=pltpu.CompilerParams(vmem_limit_bytes=VMEM),
        name="pack_one",
        cost_estimate=cost(3),
    )(jnp.stack([block, jnp.int32(blocks)]), movie, movie, movie)


def pack_kernel(tiles, skip, me_ref, movie_ref, above_ref, below_ref, *refs):
    outs, rest, pivot, values = list(refs[:-3]), refs[-3], refs[-2], refs[-1]
    frames, rows, width = movie_ref.shape
    stride = rows + PAD
    count = width // LANES
    blocks = count // tiles
    zero = jnp.zeros((frames * stride, LANES), jnp.float32)
    values[0] = zero
    values[count + 1] = zero
    for t in range(count):
        lanes = slice(t * LANES, (t + 1) * LANES)
        lay_out(
            values,
            t + 1,
            movie_ref[:, :, lanes],
            above_ref[:, :, lanes],
            below_ref[:, :, lanes],
        )
    places = []
    for k in range(blocks):
        first = 1 + (me_ref[0] ^ k) * tiles
        places.append(([first + t for t in range(tiles)], first - 1, first + tiles))
    kept = [k for k in range(blocks) if k != skip]
    write_packed(values, [places[k] for k in kept], rows, 0, outs)

    own, left, right = places[skip]
    edge = jnp.zeros((PAIR, LANES), jnp.float32)
    for n, row in enumerate((0, rows + REACH)):
        for t, place in enumerate(own):
            both = both_rows(values, place, row, stride)
            start = (t * 2 + n) * PAIR
            rest[start : start + PAIR, :] = both.astype(jnp.bfloat16)
        edge = folded_in(edge, edge_sides(values, left, right, row, stride), n)
    rest[tiles * 2 * PAIR :, :] = edge.astype(jnp.bfloat16)

    own, left, right = places[0]
    lane = lax.broadcasted_iota(jnp.int32, (PAIR, LANES), 1)

    def first_frame(place, row):
        parts = [
            jnp.broadcast_to(values[place, pl.ds(row + j, 1), :], (GROUP, LANES))
            for j in range(2)
        ]
        return jnp.concatenate(parts, axis=0)

    def pair(q, carry):
        at = pl.ds(pl.multiple_of(q * PAIR, PAIR), PAIR)
        for t, place in enumerate(own):
            pivot[t, at, :] = first_frame(place, 2 * q).astype(jnp.bfloat16)
        sides = jnp.where(
            lane >= LANES - REACH, first_frame(left, 2 * q), first_frame(right, 2 * q)
        )
        pivot[tiles, at, :] = sides.astype(jnp.bfloat16)
        return carry

    lax.fori_loop(0, rows // 2 + 2, pair, 0, unroll=2)


def pack_rest(movie, above, below, me, blocks, skip):
    frames, rows, width = movie.shape
    tiles = width // blocks // LANES
    length = tiles * (rows + 2 * REACH) * GROUP + folded_pairs(rows // 2 + 2) * PAIR
    whole = pl.BlockSpec(memory_space=pltpu.VMEM)
    kept = [k for k in range(blocks) if k != skip]
    shapes = [(length, LANES)] * len(kept)
    shapes += [((tiles * 2 + 1) * PAIR, LANES)]
    shapes += [(tiles + 1, (rows + 2 * REACH) * GROUP, LANES)]
    results = pl.pallas_call(
        lambda *refs: pack_kernel(tiles, skip, *refs),
        out_shape=[jax.ShapeDtypeStruct(shape, jnp.bfloat16) for shape in shapes],
        in_specs=[pl.BlockSpec(memory_space=pltpu.SMEM)] + [whole] * 3,
        out_specs=[whole] * len(shapes),
        scratch_shapes=[
            pltpu.VMEM((width // LANES + 2, frames * (rows + PAD), LANES), jnp.float32)
        ],
        compiler_params=pltpu.CompilerParams(vmem_limit_bytes=VMEM),
        name="pack_rest",
        cost_estimate=cost(5),
    )(me[None], movie, above, below)
    return dict(zip(kept, results)), results[-2], results[-1]


def unfolded(edge, index):
    shift = 2 * LANES - 2 * REACH * index - REACH
    return pltpu.roll(edge, lax.rem(shift, LANES), 1)


def unfold_edges(tiles, rows, block, edges, i):
    pairs = rows // 2 + 2

    def put(q, edge, index):
        start = q * PAIR
        if not isinstance(start, int):
            start = pl.multiple_of(start, PAIR)
        edges[i, pl.ds(start, PAIR), :] = unfolded(edge, index).astype(jnp.bfloat16)

    def tile_of(ref, start):
        return ref[start : start + PAIR, :].astype(jnp.float32)

    body = block[0]
    if len(block) > 1:
        around = tile_of(block[1], tiles * 2 * PAIR)
        put(0, around, 0)
        put(pairs - 1, around, 1)
        pairs, lead = rows // 2, 1
    else:
        lead = 0
    for part in range(folded_pairs(pairs)):
        edge = tile_of(body, (tiles * pairs + part) * PAIR)

        def fill(q, carry, part=part, edge=edge):
            put(q + lead, edge, q - part * FOLD)
            return carry

        first, last = part * FOLD, min((part + 1) * FOLD, pairs)
        unroll = 8 if (last - first) % 8 == 0 else 1
        lax.fori_loop(first, last, fill, 0, unroll=unroll)


def merged(first, second, distance):
    row = lax.broadcasted_iota(jnp.int32, first.shape, 0)
    low = (row & distance) == 0
    kept = jnp.where(low, first, second)
    moved = jnp.where(low, second, first)
    return kept + pltpu.roll(moved, GROUP - distance, 0)


def lag_kernel(tiles, rows, frames, counts, has_prior, last, *refs):
    refs = list(refs)
    pivot_ref = refs[0]
    refs = refs[1:]
    sources = len(counts)
    blocks = []
    for count in counts:
        blocks.append(refs[:count])
        refs = refs[count:]
    prior = None
    if has_prior:
        prior, prior_sum = refs[:2]
        refs = refs[2:]
    if last:
        out, edges, rings, shifts, staged, sums, means, cov, sems = refs
    else:
        maps, sums, edges, rings, shifts = refs
    ring = tiles + 1
    span = (rows + 2 * REACH) * GROUP

    for i, block in enumerate(blocks):
        unfold_edges(tiles, rows, block, edges, i)
        if len(block) > 1:
            body, around = block
            for t in range(tiles):
                start = t * rows * GROUP
                rings[t, PAIR : span - PAIR, :] = body[start : start + rows * GROUP, :]
                start = t * 2 * PAIR
                rings[t, :PAIR, :] = around[start : start + PAIR, :]
                rings[t, span - PAIR :, :] = around[start + PAIR : start + 2 * PAIR, :]

    def raw_values(i, t, start, size):
        if t == tiles:
            return edges[i, pl.ds(start, size), :]
        if len(blocks[i]) > 1:
            return rings[t, pl.ds(start, size), :]
        start = pl.multiple_of(t * span + start, PAIR)
        return blocks[i][0][pl.ds(start, size), :]

    source = lax.broadcasted_iota(jnp.int32, (2 * LANES, LANES), 0)
    target = lax.broadcasted_iota(jnp.int32, (2 * LANES, LANES), 1)
    moves = jnp.concatenate(
        [jnp.where(source == target + b, 1.0, 0.0) for b in range(1, REACH + 1)], axis=1
    ).astype(jnp.bfloat16)
    size = span // (2 if sources < 3 else 17)
    if size % PAIR or span % size:
        size = PAIR

    def spread(c, carry):
        start = pl.multiple_of(c * size, PAIR)
        at = pl.ds(start, size)
        raw = [[pivot_ref[t, at, :] for t in range(ring)]]
        for i in range(sources):
            raw.append([raw_values(i, t, start, size) for t in range(ring)])
        wide = jnp.concatenate(
            [
                jnp.concatenate([r[t], r[(t + 1) % ring]], axis=1)
                for r in raw
                for t in range(ring)
            ],
            axis=0,
        )
        moved = jnp.dot(wide, moves, preferred_element_type=jnp.float32)

        def version(i, t, b):
            if b == 0:
                return raw[i][t].astype(jnp.float32)
            first = (i * ring + t) * size
            return moved[first : first + size, (b - 1) * LANES : b * LANES]

        for t in range(ring):
            for b in range(REACH + 1):
                pivot = version(0, t, b)
                for i in range(1, sources + 1):
                    shifts[b, i - 1, t, at, :] = version(i, t, b) - pivot
        return carry

    lax.fori_loop(0, span // size, spread, 0)

    def value(i, t, slot, b):
        start = slot * GROUP
        if not isinstance(start, int):
            start = pl.multiple_of(start, GROUP)
        return shifts[b, i, t, pl.ds(start, GROUP), :]

    def over_blocks(term):
        total = term(0)
        for i in range(1, sources):
            total = total + term(i)
        return total

    def fold_rows(parts):
        distance = 1
        while len(parts) > 1:
            parts = [merged(x, y, distance) for x, y in zip(parts[::2], parts[1::2])]
            distance *= 2
        return parts[0]

    def fold_two(first, second):
        total = merged(first, second, 1)
        total = total + pltpu.roll(total, GROUP - 2, 0)
        return total + pltpu.roll(total, GROUP // 2, 0)

    for t in range(ring):

        def put_sum(at, total, t=t):
            if has_prior:
                total = total + prior_sum[t, at, :]
            sums[t, at, :] = total

        def row_sum(slot, t=t):
            return over_blocks(lambda i: value(i, t, slot, 0))

        put_sum(slice(0, GROUP), fold_two(row_sum(0), row_sum(1)))
        put_sum(
            slice(rows + GROUP, rows + 2 * GROUP),
            fold_two(row_sum(rows + REACH), row_sum(rows + REACH + 1)),
        )

        def sum_rows(g, carry, t=t):
            total = fold_rows([row_sum(g * GROUP + REACH + j) for j in range(GROUP)])
            put_sum(pl.ds(pl.multiple_of((g + 1) * GROUP, GROUP), GROUP), total)
            return carry

        lax.fori_loop(0, rows // GROUP, sum_rows, 0, unroll=2)

    scale = 1.0 / frames
    sublane = lax.broadcasted_iota(jnp.int32, (GROUP, LANES), 0)
    if last:

        def spread_sums(g, carry):
            at = pl.ds(pl.multiple_of(g * GROUP, GROUP), GROUP)
            after = pl.ds(pl.multiple_of((g + 1) * GROUP, GROUP), GROUP)
            for a in range(REACH + 1):
                row_ring = [sums[t, at, :] for t in range(ring)]
                if a > 0:
                    row_ring = [
                        pltpu.roll(
                            jnp.where(sublane < a, sums[t, after, :], row), GROUP - a, 0
                        )
                        for t, row in enumerate(row_ring)
                    ]
                for t in range(ring):
                    for b in range(REACH + 1):
                        means[a, b, t, at, :] = shifted(row_ring, t, b)
            return carry

        lax.fori_loop(0, rows // GROUP + 1, spread_sums, 0)

    def put_map(k, t, at, total):
        a, b = LAG_LIST[k]
        if has_prior:
            total = total + prior[k, t, at, :]
        if last:
            here, there = means[0, max(-b, 0), t, at, :], means[a, max(b, 0), t, at, :]
            cov[k, t, at, :] = (total - here * scale * there) * scale
        else:
            maps[k, t, at, :] = total

    half = GROUP // 2
    wanted = [
        [k for k, (a, b) in enumerate(LAG_LIST) if t < tiles or b != 0]
        for t in range(ring)
    ]

    def product(i, t, slot, k):
        a, b = LAG_LIST[k]
        return value(i, t, slot, max(-b, 0)) * value(i, t, slot + a, max(b, 0))

    for t in range(ring):
        for k in wanted[t]:
            if LAG_LIST[k][0] > 0:
                first, second = [
                    over_blocks(lambda i, j=j: product(i, t, j, k)) for j in range(2)
                ]
                put_map(k, t, slice(0, GROUP), fold_two(first, second))

    def products(t, g):
        at = pl.ds(pl.multiple_of((g + 1) * GROUP, GROUP), GROUP)
        for a in range(REACH + 1):
            chosen = [k for k in wanted[t] if LAG_LIST[k][0] == a]
            folds = {k: [] for k in chosen}
            for h in range(2):
                slots = [g * GROUP + REACH + h * half + j for j in range(half)]
                totals = {k: [None] * half for k in chosen}
                for i in range(sources):
                    for k in chosen:
                        for j, slot in enumerate(slots):
                            part = product(i, t, slot, k)
                            if i > 0:
                                part = totals[k][j] + part
                            totals[k][j] = part
                for k in chosen:
                    x = merged(totals[k][0], totals[k][1], 1)
                    y = merged(totals[k][2], totals[k][3], 1)
                    folds[k].append(merged(x, y, 2))
            for k in chosen:
                put_map(k, t, at, merged(folds[k][0], folds[k][1], 4))

    def place(g):
        return pl.ds(pl.multiple_of(g * GROUP, GROUP), GROUP)

    def write(g):
        side = 2 * REACH + 1
        for k, (a, b) in enumerate(LAG_LIST):
            index = side * (a + REACH) + b + REACH
            mirror = side**2 - 1 - index
            for n, rise, offset in ((index, 0, min(b, 0)), (mirror, a, min(-b, 0))):
                row_ring = [
                    cov[k, t, place(g + 1), :] if t < tiles or offset else None
                    for t in range(ring)
                ]
                if rise > 0:
                    row_ring = [
                        row
                        if row is None
                        else pltpu.roll(
                            jnp.where(
                                sublane >= GROUP - rise, cov[k, t, place(g), :], row
                            ),
                            rise,
                            0,
                        )
                        for t, row in enumerate(row_ring)
                    ]
                for t in range(tiles):
                    lanes = slice(t * LANES, (t + 1) * LANES)
                    staged[n, place(g), lanes] = shifted(row_ring, t, offset)
                if index == mirror:
                    break

    def copy_out(g):
        rows_of = place(g)
        return pltpu.make_async_copy(
            staged.at[:, rows_of, :], out.at[:, rows_of, :], sems.at[g]
        )

    half_groups = rows // GROUP // 2
    for first in (0, half_groups):

        def sum_eight(g, carry):
            for t in range(ring):
                products(t, g)
            return carry

        lax.fori_loop(first, first + half_groups, sum_eight, 0)
        if last:

            def write_eight(g, carry):
                write(g)
                copy_out(g).start()
                return carry

            lax.fori_loop(first, first + half_groups, write_eight, 0)
    if last:

        def finish(g, carry):
            copy_out(g).wait()
            return carry

        lax.fori_loop(0, rows // GROUP, finish, 0)


def room(*parts):
    total = 0
    for leaf in jax.tree.leaves(parts):
        if hasattr(leaf, "shape") and jnp.issubdtype(leaf.dtype, jnp.floating):
            total += math.prod(leaf.shape) * jnp.dtype(leaf.dtype).itemsize
    return total * 5 // 4 + 4 * 1024 * 1024


def lag_sums(pivot, blocks, rows, tiles, frames, prior=None, last=False):
    sources = len(blocks)
    counts = [len(block) for block in blocks]
    ring = tiles + 1
    span = (rows + 2 * REACH) * GROUP
    operands = [pivot] + [a for block in blocks for a in block] + list(prior or ())
    whole = pl.BlockSpec(memory_space=pltpu.VMEM)
    map_shape = (len(LAG_LIST), ring, rows + GROUP, LANES)
    sum_shape = (ring, rows + 2 * GROUP, LANES)
    scratch = [
        pltpu.VMEM((sources, span, LANES), jnp.bfloat16),
        pltpu.VMEM((tiles, span, LANES), jnp.bfloat16),
        pltpu.VMEM((REACH + 1, sources, ring, span, LANES), jnp.float32),
    ]
    if last:
        shape = ((2 * REACH + 1) ** 2, rows, tiles * LANES)
        out_shape = jax.ShapeDtypeStruct(shape, jnp.float32)
        out_specs = pl.BlockSpec(memory_space=pl.ANY)
        scratch += [
            pltpu.VMEM(shape, jnp.float32),
            pltpu.VMEM(sum_shape, jnp.float32),
            pltpu.VMEM((REACH + 1,) * 2 + (ring, rows + GROUP, LANES), jnp.float32),
            pltpu.VMEM(map_shape, jnp.float32),
            pltpu.SemaphoreType.DMA((rows // GROUP,)),
        ]
    else:
        out_shape = (
            jax.ShapeDtypeStruct(map_shape, jnp.float32),
            jax.ShapeDtypeStruct(sum_shape, jnp.float32),
        )
        out_specs = (whole, whole)
    return pl.pallas_call(
        lambda *refs: lag_kernel(
            tiles, rows, frames, counts, prior is not None, last, *refs
        ),
        out_shape=out_shape,
        in_specs=[whole] * len(operands),
        out_specs=out_specs,
        scratch_shapes=scratch,
        compiler_params=pltpu.CompilerParams(
            vmem_limit_bytes=room(scratch, operands, out_shape)
        ),
        name="lag_maps" if last else "lag_sums",
        cost_estimate=cost(2 + 2 * sources),
    )(*operands)


def body(movie):
    frames_here, rows, width = movie.shape
    peers = lax.axis_size("frame")
    tiles = width // peers // LANES
    me = lax.axis_index("frame")
    frames = frames_here * peers
    half = peers // 2
    far = list(range(half, peers))
    near = list(range(1, half))
    strips = lax.axis_size("strip")
    up = [(i, i + 1) for i in range(strips - 1)]
    down = [(j, i) for i, j in up]
    moved = {}

    def send(k, payload, after=None):
        if after is not None:
            payload, moved[after] = lax.optimization_barrier((payload, moved[after]))
        moved[k] = lax.ppermute(payload, "frame", [(i, i ^ k) for i in range(peers)])

    ahead = pack_one(movie, me ^ far[0], peers)
    send(far[0], ahead)
    last, initial = movie[:, rows - REACH :, :], movie[:, :REACH, :]
    above = lax.ppermute(last, "strip", up)
    below = lax.ppermute(initial, "strip", down)
    packed, rest, pivot = pack_rest(movie, above, below, me, peers, far[0])
    rest, moved[far[0]] = lax.optimization_barrier((rest, moved[far[0]]))
    around = lax.ppermute(rest, "frame", [(i, i ^ far[0]) for i in range(peers)])
    for k in far[1:2] + near:
        send(k, packed[k], far[0])
    for n, k in enumerate(far[2:]):
        send(k, packed[k], near[n % len(near)])

    def sums(group, prior=None, last=False):
        blocks = [(moved[k], around) if k == far[0] else (moved[k],) for k in group]
        return lag_sums(pivot, blocks, rows, tiles, frames, prior, last)

    moved[0] = packed[0]
    prior = sums([0] + far[:1] + near[:-1])
    prior = sums(near[-1:] + far[1:-2], prior)
    prior = sums(far[-2:-1], prior)
    return sums(far[-1:], prior, True)


def solution(mesh):
    return jax.shard_map(
        body,
        mesh=mesh,
        in_specs=(P("frame", "strip", None),),
        out_specs=P(None, "strip", "frame"),
        check_vma=False,
    )
```

```python
import math

import jax
import jax.numpy as jnp
from jax import lax
from jax.experimental import pallas as pl
from jax.experimental.pallas import tpu as pltpu
from jax.sharding import PartitionSpec as P

REACH = 2
LANES = 128
GROUP = 8
FOLD = LANES // (2 * REACH)
PAD = 2 * REACH
PAIR = 2 * GROUP
LAG_LIST = tuple(
    (a, b)
    for a in range(REACH + 1)
    for b in range(-REACH, REACH + 1)
    if a > 0 or b >= 0
)
def cost(micros):
    work = int(micros * 1e9 * 0.3)
    return pl.CostEstimate(flops=work, bytes_accessed=work // 300, transcendentals=0)


VMEM = 56 * 1024 * 1024


def shifted(ring, index, offset):
    tile = ring[index]
    if offset == 0:
        return tile
    lane = lax.broadcasted_iota(jnp.int32, tile.shape, tile.ndim - 1)
    if offset > 0:
        other = ring[(index + 1) % len(ring)]
        mixed = jnp.where(lane < offset, other, tile)
    else:
        other = ring[index - 1]
        mixed = jnp.where(lane >= LANES + offset, other, tile)
    return pltpu.roll(mixed, (-offset) % LANES, 1)


def folded_pairs(pairs):
    return -(-pairs // FOLD)


def both_rows(ref, index, row, stride):
    return jnp.concatenate(
        [ref[index, pl.ds(row + j, GROUP, stride=stride), :] for j in range(2)], axis=0
    )


def lay_out(ref, place, value, above=None, below=None):
    frames, rows, _ = value.shape
    for f in range(frames):
        start = f * (rows + PAD)
        ref[place, start + REACH : start + REACH + rows, :] = value[f].astype(jnp.float32)
        if above is not None:
            ref[place, start : start + REACH, :] = above[f].astype(jnp.float32)
            end = start + REACH + rows
            ref[place, end : end + REACH, :] = below[f].astype(jnp.float32)


def edge_sides(ref, left, right, row, stride):
    lane = lax.broadcasted_iota(jnp.int32, (PAIR, LANES), 1)
    return jnp.where(
        lane >= LANES - REACH,
        both_rows(ref, left, row, stride),
        both_rows(ref, right, row, stride),
    )


def folded_in(edge, sides, index):
    lane = lax.broadcasted_iota(jnp.int32, (PAIR, LANES), 1)
    first = 2 * REACH * index
    placed = pltpu.roll(sides, first + REACH, 1)
    return jnp.where((lane >= first) & (lane < first + 2 * REACH), placed, edge)


def write_packed(ref, places, rows, offset, outs):
    stride = rows + PAD
    pairs = outs_pairs = rows // 2 + (2 if offset == 0 else 0)
    span = pairs * PAIR
    zero = jnp.zeros((PAIR, LANES), jnp.float32)
    for part in range(folded_pairs(pairs)):

        def pair(q, edges, part=part):
            row = offset + 2 * q
            result = []
            for (own, left, right), out, edge in zip(places, outs, edges):
                for t, place in enumerate(own):
                    start = pl.multiple_of(t * span + q * PAIR, PAIR)
                    both = both_rows(ref, place, row, stride)
                    out[pl.ds(start, PAIR), :] = both.astype(jnp.bfloat16)
                sides = edge_sides(ref, left, right, row, stride)
                result.append(folded_in(edge, sides, q - part * FOLD))
            return tuple(result)

        first, last = part * FOLD, min((part + 1) * FOLD, outs_pairs)
        unroll = 4 if (last - first) % 4 == 0 else 1
        edges = lax.fori_loop(first, last, pair, (zero,) * len(outs), unroll=unroll)
        for (own, _, _), out, edge in zip(places, outs, edges):
            start = len(own) * span + part * PAIR
            out[start : start + PAIR, :] = edge.astype(jnp.bfloat16)


def pack_one_kernel(tiles, block_ref, main_ref, left_ref, right_ref, out_ref, values):
    rows = main_ref.shape[1]
    block, blocks = block_ref[0], block_ref[1]
    for t in range(tiles):
        lay_out(values, t, main_ref[:, :, t * LANES : (t + 1) * LANES])
    lay_out(values, tiles, left_ref[...])
    lay_out(values, tiles + 1, right_ref[...])

    @pl.when(block == 0)
    def _():
        values[tiles] = jnp.zeros(values.shape[1:], jnp.float32)

    @pl.when(block == blocks - 1)
    def _():
        values[tiles + 1] = jnp.zeros(values.shape[1:], jnp.float32)

    places = [(list(range(tiles)), tiles, tiles + 1)]
    write_packed(values, places, rows, REACH, [out_ref])


def packed_length(rows, tiles):
    return tiles * rows * GROUP + folded_pairs(rows // 2) * PAIR


def pack_one(movie, block, blocks):
    frames, rows, width = movie.shape
    columns = width // blocks
    tiles = columns // LANES
    last = width // LANES - 1
    length = packed_length(rows, tiles)
    return pl.pallas_call(
        lambda *refs: pack_one_kernel(tiles, *refs),
        out_shape=jax.ShapeDtypeStruct((length, LANES), jnp.bfloat16),
        grid_spec=pltpu.PrefetchScalarGridSpec(
            num_scalar_prefetch=1,
            grid=(1,),
            in_specs=[
                pl.BlockSpec((frames, rows, columns), lambda i, s: (0, 0, s[0])),
                pl.BlockSpec(
                    (frames, rows, LANES),
                    lambda i, s: (0, 0, jnp.maximum(s[0] * tiles - 1, 0)),
                ),
                pl.BlockSpec(
                    (frames, rows, LANES),
                    lambda i, s: (0, 0, jnp.minimum(s[0] * tiles + tiles, last)),
                ),
            ],
            out_specs=pl.BlockSpec((length, LANES), lambda i, s: (0, 0)),
            scratch_shapes=[
                pltpu.VMEM((tiles + 2, frames * (rows + PAD), LANES), jnp.float32)
            ],
        ),
        compiler_params=pltpu.CompilerParams(vmem_limit_bytes=VMEM),
        name="pack_one",
        cost_estimate=cost(3),
    )(jnp.stack([block, jnp.int32(blocks)]), movie, movie, movie)


def pack_kernel(tiles, skip, me_ref, movie_ref, above_ref, below_ref, *refs):
    outs, rest, pivot, values = list(refs[:-3]), refs[-3], refs[-2], refs[-1]
    frames, rows, width = movie_ref.shape
    stride = rows + PAD
    count = width // LANES
    blocks = count // tiles
    zero = jnp.zeros((frames * stride, LANES), jnp.float32)
    values[0] = zero
    values[count + 1] = zero
    for t in range(count):
        lanes = slice(t * LANES, (t + 1) * LANES)
        lay_out(
            values,
            t + 1,
            movie_ref[:, :, lanes],
            above_ref[:, :, lanes],
            below_ref[:, :, lanes],
        )
    places = []
    for k in range(blocks):
        first = 1 + (me_ref[0] ^ k) * tiles
        places.append(([first + t for t in range(tiles)], first - 1, first + tiles))
    kept = [k for k in range(blocks) if k != skip]
    write_packed(values, [places[k] for k in kept], rows, 0, outs)

    own, left, right = places[skip]
    edge = jnp.zeros((PAIR, LANES), jnp.float32)
    for n, row in enumerate((0, rows + REACH)):
        for t, place in enumerate(own):
            both = both_rows(values, place, row, stride)
            start = (t * 2 + n) * PAIR
            rest[start : start + PAIR, :] = both.astype(jnp.bfloat16)
        edge = folded_in(edge, edge_sides(values, left, right, row, stride), n)
    rest[tiles * 2 * PAIR :, :] = edge.astype(jnp.bfloat16)

    own, left, right = places[0]
    lane = lax.broadcasted_iota(jnp.int32, (PAIR, LANES), 1)

    def first_frame(place, row):
        parts = [
            jnp.broadcast_to(values[place, pl.ds(row + j, 1), :], (GROUP, LANES))
            for j in range(2)
        ]
        return jnp.concatenate(parts, axis=0)

    def pair(q, carry):
        at = pl.ds(pl.multiple_of(q * PAIR, PAIR), PAIR)
        for t, place in enumerate(own):
            pivot[t, at, :] = first_frame(place, 2 * q).astype(jnp.bfloat16)
        sides = jnp.where(
            lane >= LANES - REACH, first_frame(left, 2 * q), first_frame(right, 2 * q)
        )
        pivot[tiles, at, :] = sides.astype(jnp.bfloat16)
        return carry

    lax.fori_loop(0, rows // 2 + 2, pair, 0, unroll=2)


def pack_rest(movie, above, below, me, blocks, skip):
    frames, rows, width = movie.shape
    tiles = width // blocks // LANES
    length = tiles * (rows + 2 * REACH) * GROUP + folded_pairs(rows // 2 + 2) * PAIR
    whole = pl.BlockSpec(memory_space=pltpu.VMEM)
    kept = [k for k in range(blocks) if k != skip]
    shapes = [(length, LANES)] * len(kept)
    shapes += [((tiles * 2 + 1) * PAIR, LANES)]
    shapes += [(tiles + 1, (rows + 2 * REACH) * GROUP, LANES)]
    results = pl.pallas_call(
        lambda *refs: pack_kernel(tiles, skip, *refs),
        out_shape=[jax.ShapeDtypeStruct(shape, jnp.bfloat16) for shape in shapes],
        in_specs=[pl.BlockSpec(memory_space=pltpu.SMEM)] + [whole] * 3,
        out_specs=[whole] * len(shapes),
        scratch_shapes=[
            pltpu.VMEM((width // LANES + 2, frames * (rows + PAD), LANES), jnp.float32)
        ],
        compiler_params=pltpu.CompilerParams(vmem_limit_bytes=VMEM),
        name="pack_rest",
        cost_estimate=cost(5),
    )(me[None], movie, above, below)
    return dict(zip(kept, results)), results[-2], results[-1]


def unfolded(edge, index):
    shift = 2 * LANES - 2 * REACH * index - REACH
    return pltpu.roll(edge, lax.rem(shift, LANES), 1)


def unfold_edges(tiles, rows, block, edges, i):
    pairs = rows // 2 + 2

    def put(q, edge, index):
        start = q * PAIR
        if not isinstance(start, int):
            start = pl.multiple_of(start, PAIR)
        edges[i, pl.ds(start, PAIR), :] = unfolded(edge, index).astype(jnp.bfloat16)

    def tile_of(ref, start):
        return ref[start : start + PAIR, :].astype(jnp.float32)

    body = block[0]
    if len(block) > 1:
        around = tile_of(block[1], tiles * 2 * PAIR)
        put(0, around, 0)
        put(pairs - 1, around, 1)
        pairs, lead = rows // 2, 1
    else:
        lead = 0
    for part in range(folded_pairs(pairs)):
        edge = tile_of(body, (tiles * pairs + part) * PAIR)

        def fill(q, carry, part=part, edge=edge):
            put(q + lead, edge, q - part * FOLD)
            return carry

        first, last = part * FOLD, min((part + 1) * FOLD, pairs)
        unroll = 8 if (last - first) % 8 == 0 else 1
        lax.fori_loop(first, last, fill, 0, unroll=unroll)


def merged(first, second, distance):
    row = lax.broadcasted_iota(jnp.int32, first.shape, 0)
    low = (row & distance) == 0
    kept = jnp.where(low, first, second)
    moved = jnp.where(low, second, first)
    return kept + pltpu.roll(moved, GROUP - distance, 0)


def lag_kernel(tiles, rows, frames, counts, has_prior, last, *refs):
    refs = list(refs)
    pivot_ref = refs[0]
    refs = refs[1:]
    sources = len(counts)
    blocks = []
    for count in counts:
        blocks.append(refs[:count])
        refs = refs[count:]
    prior = None
    if has_prior:
        prior, prior_sum = refs[:2]
        refs = refs[2:]
    if last:
        out, edges, rings, shifts, staged, sums, means, cov, sems = refs
    else:
        maps, sums, edges, rings, shifts = refs
    ring = tiles + 1
    span = (rows + 2 * REACH) * GROUP

    for i, block in enumerate(blocks):
        unfold_edges(tiles, rows, block, edges, i)
        if len(block) > 1:
            body, around = block
            for t in range(tiles):
                start = t * rows * GROUP
                rings[t, PAIR : span - PAIR, :] = body[start : start + rows * GROUP, :]
                start = t * 2 * PAIR
                rings[t, :PAIR, :] = around[start : start + PAIR, :]
                rings[t, span - PAIR :, :] = around[start + PAIR : start + 2 * PAIR, :]

    def raw_values(i, t, start, size):
        if t == tiles:
            return edges[i, pl.ds(start, size), :]
        if len(blocks[i]) > 1:
            return rings[t, pl.ds(start, size), :]
        start = pl.multiple_of(t * span + start, PAIR)
        return blocks[i][0][pl.ds(start, size), :]

    source = lax.broadcasted_iota(jnp.int32, (2 * LANES, LANES), 0)
    target = lax.broadcasted_iota(jnp.int32, (2 * LANES, LANES), 1)
    moves = jnp.concatenate(
        [jnp.where(source == target + b, 1.0, 0.0) for b in range(1, REACH + 1)], axis=1
    ).astype(jnp.bfloat16)
    size = span // (2 if sources < 3 else 17)
    if size % PAIR or span % size:
        size = PAIR

    def spread(c, carry):
        start = pl.multiple_of(c * size, PAIR)
        at = pl.ds(start, size)
        raw = [[pivot_ref[t, at, :] for t in range(ring)]]
        for i in range(sources):
            raw.append([raw_values(i, t, start, size) for t in range(ring)])
        wide = jnp.concatenate(
            [
                jnp.concatenate([r[t], r[(t + 1) % ring]], axis=1)
                for r in raw
                for t in range(ring)
            ],
            axis=0,
        )
        moved = jnp.dot(wide, moves, preferred_element_type=jnp.float32)

        def version(i, t, b):
            if b == 0:
                return raw[i][t].astype(jnp.float32)
            first = (i * ring + t) * size
            return moved[first : first + size, (b - 1) * LANES : b * LANES]

        for t in range(ring):
            for b in range(REACH + 1):
                pivot = version(0, t, b)
                for i in range(1, sources + 1):
                    shifts[b, i - 1, t, at, :] = version(i, t, b) - pivot
        return carry

    lax.fori_loop(0, span // size, spread, 0)

    def value(i, t, slot, b):
        start = slot * GROUP
        if not isinstance(start, int):
            start = pl.multiple_of(start, GROUP)
        return shifts[b, i, t, pl.ds(start, GROUP), :]

    def over_blocks(term):
        total = term(0)
        for i in range(1, sources):
            total = total + term(i)
        return total

    def fold_rows(parts):
        distance = 1
        while len(parts) > 1:
            parts = [merged(x, y, distance) for x, y in zip(parts[::2], parts[1::2])]
            distance *= 2
        return parts[0]

    def fold_two(first, second):
        total = merged(first, second, 1)
        total = total + pltpu.roll(total, GROUP - 2, 0)
        return total + pltpu.roll(total, GROUP // 2, 0)

    for t in range(ring):

        def put_sum(at, total, t=t):
            if has_prior:
                total = total + prior_sum[t, at, :]
            sums[t, at, :] = total

        def row_sum(slot, t=t):
            return over_blocks(lambda i: value(i, t, slot, 0))

        put_sum(slice(0, GROUP), fold_two(row_sum(0), row_sum(1)))
        put_sum(
            slice(rows + GROUP, rows + 2 * GROUP),
            fold_two(row_sum(rows + REACH), row_sum(rows + REACH + 1)),
        )

        def sum_rows(g, carry, t=t):
            total = fold_rows([row_sum(g * GROUP + REACH + j) for j in range(GROUP)])
            put_sum(pl.ds(pl.multiple_of((g + 1) * GROUP, GROUP), GROUP), total)
            return carry

        lax.fori_loop(0, rows // GROUP, sum_rows, 0, unroll=2)

    scale = 1.0 / frames
    sublane = lax.broadcasted_iota(jnp.int32, (GROUP, LANES), 0)
    if last:

        def spread_sums(g, carry):
            at = pl.ds(pl.multiple_of(g * GROUP, GROUP), GROUP)
            after = pl.ds(pl.multiple_of((g + 1) * GROUP, GROUP), GROUP)
            for a in range(REACH + 1):
                row_ring = [sums[t, at, :] for t in range(ring)]
                if a > 0:
                    row_ring = [
                        pltpu.roll(
                            jnp.where(sublane < a, sums[t, after, :], row), GROUP - a, 0
                        )
                        for t, row in enumerate(row_ring)
                    ]
                for t in range(ring):
                    for b in range(REACH + 1):
                        means[a, b, t, at, :] = shifted(row_ring, t, b)
            return carry

        lax.fori_loop(0, rows // GROUP + 1, spread_sums, 0)

    def put_map(k, t, at, total):
        a, b = LAG_LIST[k]
        if has_prior:
            total = total + prior[k, t, at, :]
        if last:
            here, there = means[0, max(-b, 0), t, at, :], means[a, max(b, 0), t, at, :]
            cov[k, t, at, :] = (total - here * scale * there) * scale
        else:
            maps[k, t, at, :] = total

    half = GROUP // 2
    wanted = [
        [k for k, (a, b) in enumerate(LAG_LIST) if t < tiles or b != 0]
        for t in range(ring)
    ]

    def product(i, t, slot, k):
        a, b = LAG_LIST[k]
        return value(i, t, slot, max(-b, 0)) * value(i, t, slot + a, max(b, 0))

    for t in range(ring):
        for k in wanted[t]:
            if LAG_LIST[k][0] > 0:
                first, second = [
                    over_blocks(lambda i, j=j: product(i, t, j, k)) for j in range(2)
                ]
                put_map(k, t, slice(0, GROUP), fold_two(first, second))

    def products(t, g):
        at = pl.ds(pl.multiple_of((g + 1) * GROUP, GROUP), GROUP)
        for a in range(REACH + 1):
            chosen = [k for k in wanted[t] if LAG_LIST[k][0] == a]
            folds = {k: [] for k in chosen}
            for h in range(2):
                slots = [g * GROUP + REACH + h * half + j for j in range(half)]
                totals = {k: [None] * half for k in chosen}
                for i in range(sources):
                    for k in chosen:
                        for j, slot in enumerate(slots):
                            part = product(i, t, slot, k)
                            if i > 0:
                                part = totals[k][j] + part
                            totals[k][j] = part
                for k in chosen:
                    x = merged(totals[k][0], totals[k][1], 1)
                    y = merged(totals[k][2], totals[k][3], 1)
                    folds[k].append(merged(x, y, 2))
            for k in chosen:
                put_map(k, t, at, merged(folds[k][0], folds[k][1], 4))

    def place(g):
        return pl.ds(pl.multiple_of(g * GROUP, GROUP), GROUP)

    def write(g):
        side = 2 * REACH + 1
        for k, (a, b) in enumerate(LAG_LIST):
            index = side * (a + REACH) + b + REACH
            mirror = side**2 - 1 - index
            for n, rise, offset in ((index, 0, min(b, 0)), (mirror, a, min(-b, 0))):
                row_ring = [
                    cov[k, t, place(g + 1), :] if t < tiles or offset else None
                    for t in range(ring)
                ]
                if rise > 0:
                    row_ring = [
                        row
                        if row is None
                        else pltpu.roll(
                            jnp.where(
                                sublane >= GROUP - rise, cov[k, t, place(g), :], row
                            ),
                            rise,
                            0,
                        )
                        for t, row in enumerate(row_ring)
                    ]
                for t in range(tiles):
                    lanes = slice(t * LANES, (t + 1) * LANES)
                    staged[n, place(g), lanes] = shifted(row_ring, t, offset)
                if index == mirror:
                    break

    def copy_out(g):
        rows_of = place(g)
        return pltpu.make_async_copy(
            staged.at[:, rows_of, :], out.at[:, rows_of, :], sems.at[g]
        )

    half_groups = rows // GROUP // 2
    for first in (0, half_groups):

        def sum_eight(g, carry):
            for t in range(ring):
                products(t, g)
            return carry

        lax.fori_loop(first, first + half_groups, sum_eight, 0)
        if last:

            def write_eight(g, carry):
                write(g)
                copy_out(g).start()
                return carry

            lax.fori_loop(first, first + half_groups, write_eight, 0)
    if last:

        def finish(g, carry):
            copy_out(g).wait()
            return carry

        lax.fori_loop(0, rows // GROUP, finish, 0)


def room(*parts):
    total = 0
    for leaf in jax.tree.leaves(parts):
        if hasattr(leaf, "shape") and jnp.issubdtype(leaf.dtype, jnp.floating):
            total += math.prod(leaf.shape) * jnp.dtype(leaf.dtype).itemsize
    return total * 5 // 4 + 4 * 1024 * 1024


def lag_sums(pivot, blocks, rows, tiles, frames, prior=None, last=False):
    sources = len(blocks)
    counts = [len(block) for block in blocks]
    ring = tiles + 1
    span = (rows + 2 * REACH) * GROUP
    operands = [pivot] + [a for block in blocks for a in block] + list(prior or ())
    whole = pl.BlockSpec(memory_space=pltpu.VMEM)
    map_shape = (len(LAG_LIST), ring, rows + GROUP, LANES)
    sum_shape = (ring, rows + 2 * GROUP, LANES)
    scratch = [
        pltpu.VMEM((sources, span, LANES), jnp.bfloat16),
        pltpu.VMEM((tiles, span, LANES), jnp.bfloat16),
        pltpu.VMEM((REACH + 1, sources, ring, span, LANES), jnp.float32),
    ]
    if last:
        shape = ((2 * REACH + 1) ** 2, rows, tiles * LANES)
        out_shape = jax.ShapeDtypeStruct(shape, jnp.float32)
        out_specs = pl.BlockSpec(memory_space=pl.ANY)
        scratch += [
            pltpu.VMEM(shape, jnp.float32),
            pltpu.VMEM(sum_shape, jnp.float32),
            pltpu.VMEM((REACH + 1,) * 2 + (ring, rows + GROUP, LANES), jnp.float32),
            pltpu.VMEM(map_shape, jnp.float32),
            pltpu.SemaphoreType.DMA((rows // GROUP,)),
        ]
    else:
        out_shape = (
            jax.ShapeDtypeStruct(map_shape, jnp.float32),
            jax.ShapeDtypeStruct(sum_shape, jnp.float32),
        )
        out_specs = (whole, whole)
    return pl.pallas_call(
        lambda *refs: lag_kernel(
            tiles, rows, frames, counts, prior is not None, last, *refs
        ),
        out_shape=out_shape,
        in_specs=[whole] * len(operands),
        out_specs=out_specs,
        scratch_shapes=scratch,
        compiler_params=pltpu.CompilerParams(
            vmem_limit_bytes=room(scratch, operands, out_shape)
        ),
        name="lag_maps" if last else "lag_sums",
        cost_estimate=cost(2 + 2 * sources),
    )(*operands)


def body(movie):
    frames_here, rows, width = movie.shape
    peers = lax.axis_size("frame")
    tiles = width // peers // LANES
    me = lax.axis_index("frame")
    frames = frames_here * peers
    half = peers // 2
    far = list(range(half, peers))
    near = list(range(1, half))
    strips = lax.axis_size("strip")
    up = [(i, i + 1) for i in range(strips - 1)]
    down = [(j, i) for i, j in up]
    moved = {}

    def send(k, payload, after=None):
        if after is not None:
            payload, moved[after] = lax.optimization_barrier((payload, moved[after]))
        moved[k] = lax.ppermute(payload, "frame", [(i, i ^ k) for i in range(peers)])

    ahead = pack_one(movie, me ^ far[0], peers)
    send(far[0], ahead)
    last, initial = movie[:, rows - REACH :, :], movie[:, :REACH, :]
    above = lax.ppermute(last, "strip", up)
    below = lax.ppermute(initial, "strip", down)
    packed, rest, pivot = pack_rest(movie, above, below, me, peers, far[0])
    rest, moved[far[0]] = lax.optimization_barrier((rest, moved[far[0]]))
    around = lax.ppermute(rest, "frame", [(i, i ^ far[0]) for i in range(peers)])
    for k in far[1:2] + near:
        send(k, packed[k], far[0])
    for n, k in enumerate(far[2:]):
        send(k, packed[k], far[1] if n == 0 else near[0])

    def sums(group, prior=None, last=False):
        blocks = [(moved[k], around) if k == far[0] else (moved[k],) for k in group]
        return lag_sums(pivot, blocks, rows, tiles, frames, prior, last)

    moved[0] = packed[0]
    prior = sums([0] + far[:1] + near[:-1])
    prior = sums(near[-1:] + far[1:-1], prior)
    return sums(far[-1:], prior, True)


def solution(mesh):
    return jax.shard_map(
        body,
        mesh=mesh,
        in_specs=(P("frame", "strip", None),),
        out_specs=P(None, "strip", "frame"),
        check_vma=False,
    )
```

```python
import math

import jax
import jax.numpy as jnp
from jax import lax
from jax.experimental import pallas as pl
from jax.experimental.pallas import tpu as pltpu
from jax.sharding import PartitionSpec as P

REACH = 2
LANES = 128
GROUP = 8
FOLD = LANES // (2 * REACH)
PAD = 2 * REACH
PAIR = 2 * GROUP
LAG_LIST = tuple(
    (a, b)
    for a in range(REACH + 1)
    for b in range(-REACH, REACH + 1)
    if a > 0 or b >= 0
)
def cost(micros):
    work = int(micros * 1e9 * 0.3)
    return pl.CostEstimate(flops=work, bytes_accessed=work // 300, transcendentals=0)


VMEM = 56 * 1024 * 1024


def shifted(ring, index, offset):
    tile = ring[index]
    if offset == 0:
        return tile
    lane = lax.broadcasted_iota(jnp.int32, tile.shape, tile.ndim - 1)
    if offset > 0:
        other = ring[(index + 1) % len(ring)]
        mixed = jnp.where(lane < offset, other, tile)
    else:
        other = ring[index - 1]
        mixed = jnp.where(lane >= LANES + offset, other, tile)
    return pltpu.roll(mixed, (-offset) % LANES, 1)


def folded_pairs(pairs):
    return -(-pairs // FOLD)


def both_rows(ref, index, row, stride):
    return jnp.concatenate(
        [ref[index, pl.ds(row + j, GROUP, stride=stride), :] for j in range(2)], axis=0
    )


def lay_out(ref, place, value, above=None, below=None):
    frames, rows, _ = value.shape
    for f in range(frames):
        start = f * (rows + PAD)
        ref[place, start + REACH : start + REACH + rows, :] = value[f].astype(jnp.float32)
        if above is not None:
            ref[place, start : start + REACH, :] = above[f].astype(jnp.float32)
            end = start + REACH + rows
            ref[place, end : end + REACH, :] = below[f].astype(jnp.float32)


def edge_sides(ref, left, right, row, stride):
    lane = lax.broadcasted_iota(jnp.int32, (PAIR, LANES), 1)
    return jnp.where(
        lane >= LANES - REACH,
        both_rows(ref, left, row, stride),
        both_rows(ref, right, row, stride),
    )


def folded_in(edge, sides, index):
    lane = lax.broadcasted_iota(jnp.int32, (PAIR, LANES), 1)
    first = 2 * REACH * index
    placed = pltpu.roll(sides, first + REACH, 1)
    return jnp.where((lane >= first) & (lane < first + 2 * REACH), placed, edge)


def write_packed(ref, places, rows, offset, outs):
    stride = rows + PAD
    pairs = outs_pairs = rows // 2 + (2 if offset == 0 else 0)
    span = pairs * PAIR
    zero = jnp.zeros((PAIR, LANES), jnp.float32)
    for part in range(folded_pairs(pairs)):

        def pair(q, edges, part=part):
            row = offset + 2 * q
            result = []
            for (own, left, right), out, edge in zip(places, outs, edges):
                for t, place in enumerate(own):
                    start = pl.multiple_of(t * span + q * PAIR, PAIR)
                    both = both_rows(ref, place, row, stride)
                    out[pl.ds(start, PAIR), :] = both.astype(jnp.bfloat16)
                sides = edge_sides(ref, left, right, row, stride)
                result.append(folded_in(edge, sides, q - part * FOLD))
            return tuple(result)

        first, last = part * FOLD, min((part + 1) * FOLD, outs_pairs)
        unroll = 4 if (last - first) % 4 == 0 else 1
        edges = lax.fori_loop(first, last, pair, (zero,) * len(outs), unroll=unroll)
        for (own, _, _), out, edge in zip(places, outs, edges):
            start = len(own) * span + part * PAIR
            out[start : start + PAIR, :] = edge.astype(jnp.bfloat16)


def pack_one_kernel(tiles, block_ref, main_ref, left_ref, right_ref, out_ref, values):
    rows = main_ref.shape[1]
    block, blocks = block_ref[0], block_ref[1]
    for t in range(tiles):
        lay_out(values, t, main_ref[:, :, t * LANES : (t + 1) * LANES])
    lay_out(values, tiles, left_ref[...])
    lay_out(values, tiles + 1, right_ref[...])

    @pl.when(block == 0)
    def _():
        values[tiles] = jnp.zeros(values.shape[1:], jnp.float32)

    @pl.when(block == blocks - 1)
    def _():
        values[tiles + 1] = jnp.zeros(values.shape[1:], jnp.float32)

    places = [(list(range(tiles)), tiles, tiles + 1)]
    write_packed(values, places, rows, REACH, [out_ref])


def packed_length(rows, tiles):
    return tiles * rows * GROUP + folded_pairs(rows // 2) * PAIR


def pack_one(movie, block, blocks):
    frames, rows, width = movie.shape
    columns = width // blocks
    tiles = columns // LANES
    last = width // LANES - 1
    length = packed_length(rows, tiles)
    return pl.pallas_call(
        lambda *refs: pack_one_kernel(tiles, *refs),
        out_shape=jax.ShapeDtypeStruct((length, LANES), jnp.bfloat16),
        grid_spec=pltpu.PrefetchScalarGridSpec(
            num_scalar_prefetch=1,
            grid=(1,),
            in_specs=[
                pl.BlockSpec((frames, rows, columns), lambda i, s: (0, 0, s[0])),
                pl.BlockSpec(
                    (frames, rows, LANES),
                    lambda i, s: (0, 0, jnp.maximum(s[0] * tiles - 1, 0)),
                ),
                pl.BlockSpec(
                    (frames, rows, LANES),
                    lambda i, s: (0, 0, jnp.minimum(s[0] * tiles + tiles, last)),
                ),
            ],
            out_specs=pl.BlockSpec((length, LANES), lambda i, s: (0, 0)),
            scratch_shapes=[
                pltpu.VMEM((tiles + 2, frames * (rows + PAD), LANES), jnp.float32)
            ],
        ),
        compiler_params=pltpu.CompilerParams(vmem_limit_bytes=VMEM),
        name="pack_one",
        cost_estimate=cost(3),
    )(jnp.stack([block, jnp.int32(blocks)]), movie, movie, movie)


def pack_kernel(tiles, skip, me_ref, movie_ref, above_ref, below_ref, *refs):
    outs, rest, pivot, values = list(refs[:-3]), refs[-3], refs[-2], refs[-1]
    frames, rows, width = movie_ref.shape
    stride = rows + PAD
    count = width // LANES
    blocks = count // tiles
    zero = jnp.zeros((frames * stride, LANES), jnp.float32)
    values[0] = zero
    values[count + 1] = zero
    for t in range(count):
        lanes = slice(t * LANES, (t + 1) * LANES)
        lay_out(
            values,
            t + 1,
            movie_ref[:, :, lanes],
            above_ref[:, :, lanes],
            below_ref[:, :, lanes],
        )
    places = []
    for k in range(blocks):
        first = 1 + (me_ref[0] ^ k) * tiles
        places.append(([first + t for t in range(tiles)], first - 1, first + tiles))
    kept = [k for k in range(blocks) if k != skip]
    write_packed(values, [places[k] for k in kept], rows, 0, outs)

    own, left, right = places[skip]
    edge = jnp.zeros((PAIR, LANES), jnp.float32)
    for n, row in enumerate((0, rows + REACH)):
        for t, place in enumerate(own):
            both = both_rows(values, place, row, stride)
            start = (t * 2 + n) * PAIR
            rest[start : start + PAIR, :] = both.astype(jnp.bfloat16)
        edge = folded_in(edge, edge_sides(values, left, right, row, stride), n)
    rest[tiles * 2 * PAIR :, :] = edge.astype(jnp.bfloat16)

    own, left, right = places[0]
    lane = lax.broadcasted_iota(jnp.int32, (PAIR, LANES), 1)

    def first_frame(place, row):
        parts = [
            jnp.broadcast_to(values[place, pl.ds(row + j, 1), :], (GROUP, LANES))
            for j in range(2)
        ]
        return jnp.concatenate(parts, axis=0)

    def pair(q, carry):
        at = pl.ds(pl.multiple_of(q * PAIR, PAIR), PAIR)
        for t, place in enumerate(own):
            pivot[t, at, :] = first_frame(place, 2 * q).astype(jnp.bfloat16)
        sides = jnp.where(
            lane >= LANES - REACH, first_frame(left, 2 * q), first_frame(right, 2 * q)
        )
        pivot[tiles, at, :] = sides.astype(jnp.bfloat16)
        return carry

    lax.fori_loop(0, rows // 2 + 2, pair, 0, unroll=2)


def pack_rest(movie, above, below, me, blocks, skip):
    frames, rows, width = movie.shape
    tiles = width // blocks // LANES
    length = tiles * (rows + 2 * REACH) * GROUP + folded_pairs(rows // 2 + 2) * PAIR
    whole = pl.BlockSpec(memory_space=pltpu.VMEM)
    kept = [k for k in range(blocks) if k != skip]
    shapes = [(length, LANES)] * len(kept)
    shapes += [((tiles * 2 + 1) * PAIR, LANES)]
    shapes += [(tiles + 1, (rows + 2 * REACH) * GROUP, LANES)]
    results = pl.pallas_call(
        lambda *refs: pack_kernel(tiles, skip, *refs),
        out_shape=[jax.ShapeDtypeStruct(shape, jnp.bfloat16) for shape in shapes],
        in_specs=[pl.BlockSpec(memory_space=pltpu.SMEM)] + [whole] * 3,
        out_specs=[whole] * len(shapes),
        scratch_shapes=[
            pltpu.VMEM((width // LANES + 2, frames * (rows + PAD), LANES), jnp.float32)
        ],
        compiler_params=pltpu.CompilerParams(vmem_limit_bytes=VMEM),
        name="pack_rest",
        cost_estimate=cost(5),
    )(me[None], movie, above, below)
    return dict(zip(kept, results)), results[-2], results[-1]


def unfolded(edge, index):
    shift = 2 * LANES - 2 * REACH * index - REACH
    return pltpu.roll(edge, lax.rem(shift, LANES), 1)


def unfold_edges(tiles, rows, block, edges, i):
    pairs = rows // 2 + 2

    def put(q, edge, index):
        start = q * PAIR
        if not isinstance(start, int):
            start = pl.multiple_of(start, PAIR)
        edges[i, pl.ds(start, PAIR), :] = unfolded(edge, index).astype(jnp.bfloat16)

    def tile_of(ref, start):
        return ref[start : start + PAIR, :].astype(jnp.float32)

    body = block[0]
    if len(block) > 1:
        around = tile_of(block[1], tiles * 2 * PAIR)
        put(0, around, 0)
        put(pairs - 1, around, 1)
        pairs, lead = rows // 2, 1
    else:
        lead = 0
    for part in range(folded_pairs(pairs)):
        edge = tile_of(body, (tiles * pairs + part) * PAIR)

        def fill(q, carry, part=part, edge=edge):
            put(q + lead, edge, q - part * FOLD)
            return carry

        first, last = part * FOLD, min((part + 1) * FOLD, pairs)
        unroll = 8 if (last - first) % 8 == 0 else 1
        lax.fori_loop(first, last, fill, 0, unroll=unroll)


def merged(first, second, distance):
    row = lax.broadcasted_iota(jnp.int32, first.shape, 0)
    low = (row & distance) == 0
    kept = jnp.where(low, first, second)
    moved = jnp.where(low, second, first)
    return kept + pltpu.roll(moved, GROUP - distance, 0)


def lag_kernel(tiles, rows, frames, counts, has_prior, last, *refs):
    refs = list(refs)
    pivot_ref = refs[0]
    refs = refs[1:]
    sources = len(counts)
    blocks = []
    for count in counts:
        blocks.append(refs[:count])
        refs = refs[count:]
    prior = None
    if has_prior:
        prior, prior_sum = refs[:2]
        refs = refs[2:]
    if last:
        out, edges, rings, shifts, staged, sums, means, cov, sems = refs
    else:
        maps, sums, edges, rings, shifts = refs
    ring = tiles + 1
    span = (rows + 2 * REACH) * GROUP

    for i, block in enumerate(blocks):
        unfold_edges(tiles, rows, block, edges, i)
        if len(block) > 1:
            body, around = block
            for t in range(tiles):
                start = t * rows * GROUP
                rings[t, PAIR : span - PAIR, :] = body[start : start + rows * GROUP, :]
                start = t * 2 * PAIR
                rings[t, :PAIR, :] = around[start : start + PAIR, :]
                rings[t, span - PAIR :, :] = around[start + PAIR : start + 2 * PAIR, :]

    def raw_values(i, t, start, size):
        if t == tiles:
            return edges[i, pl.ds(start, size), :]
        if len(blocks[i]) > 1:
            return rings[t, pl.ds(start, size), :]
        start = pl.multiple_of(t * span + start, PAIR)
        return blocks[i][0][pl.ds(start, size), :]

    source = lax.broadcasted_iota(jnp.int32, (2 * LANES, LANES), 0)
    target = lax.broadcasted_iota(jnp.int32, (2 * LANES, LANES), 1)
    moves = jnp.concatenate(
        [jnp.where(source == target + b, 1.0, 0.0) for b in range(1, REACH + 1)], axis=1
    ).astype(jnp.bfloat16)
    size = span // (2 if sources < 3 else 17)
    if size % PAIR or span % size:
        size = PAIR

    def spread(c, carry):
        start = pl.multiple_of(c * size, PAIR)
        at = pl.ds(start, size)
        raw = [[pivot_ref[t, at, :] for t in range(ring)]]
        for i in range(sources):
            raw.append([raw_values(i, t, start, size) for t in range(ring)])
        wide = jnp.concatenate(
            [
                jnp.concatenate([r[t], r[(t + 1) % ring]], axis=1)
                for r in raw
                for t in range(ring)
            ],
            axis=0,
        )
        moved = jnp.dot(wide, moves, preferred_element_type=jnp.float32)

        def version(i, t, b):
            if b == 0:
                return raw[i][t].astype(jnp.float32)
            first = (i * ring + t) * size
            return moved[first : first + size, (b - 1) * LANES : b * LANES]

        for t in range(ring):
            for b in range(REACH + 1):
                pivot = version(0, t, b)
                for i in range(1, sources + 1):
                    shifts[b, i - 1, t, at, :] = version(i, t, b) - pivot
        return carry

    lax.fori_loop(0, span // size, spread, 0)

    def value(i, t, slot, b):
        start = slot * GROUP
        if not isinstance(start, int):
            start = pl.multiple_of(start, GROUP)
        return shifts[b, i, t, pl.ds(start, GROUP), :]

    def over_blocks(term):
        total = term(0)
        for i in range(1, sources):
            total = total + term(i)
        return total

    def fold_rows(parts):
        distance = 1
        while len(parts) > 1:
            parts = [merged(x, y, distance) for x, y in zip(parts[::2], parts[1::2])]
            distance *= 2
        return parts[0]

    def fold_two(first, second):
        total = merged(first, second, 1)
        total = total + pltpu.roll(total, GROUP - 2, 0)
        return total + pltpu.roll(total, GROUP // 2, 0)

    for t in range(ring):

        def put_sum(at, total, t=t):
            if has_prior:
                total = total + prior_sum[t, at, :]
            sums[t, at, :] = total

        def row_sum(slot, t=t):
            return over_blocks(lambda i: value(i, t, slot, 0))

        put_sum(slice(0, GROUP), fold_two(row_sum(0), row_sum(1)))
        put_sum(
            slice(rows + GROUP, rows + 2 * GROUP),
            fold_two(row_sum(rows + REACH), row_sum(rows + REACH + 1)),
        )

        def sum_rows(g, carry, t=t):
            total = fold_rows([row_sum(g * GROUP + REACH + j) for j in range(GROUP)])
            put_sum(pl.ds(pl.multiple_of((g + 1) * GROUP, GROUP), GROUP), total)
            return carry

        lax.fori_loop(0, rows // GROUP, sum_rows, 0, unroll=2)

    scale = 1.0 / frames
    sublane = lax.broadcasted_iota(jnp.int32, (GROUP, LANES), 0)
    if last:

        def spread_sums(g, carry):
            at = pl.ds(pl.multiple_of(g * GROUP, GROUP), GROUP)
            after = pl.ds(pl.multiple_of((g + 1) * GROUP, GROUP), GROUP)
            for a in range(REACH + 1):
                row_ring = [sums[t, at, :] for t in range(ring)]
                if a > 0:
                    row_ring = [
                        pltpu.roll(
                            jnp.where(sublane < a, sums[t, after, :], row), GROUP - a, 0
                        )
                        for t, row in enumerate(row_ring)
                    ]
                for t in range(ring):
                    for b in range(REACH + 1):
                        means[a, b, t, at, :] = shifted(row_ring, t, b)
            return carry

        lax.fori_loop(0, rows // GROUP + 1, spread_sums, 0)

    def put_map(k, t, at, total):
        a, b = LAG_LIST[k]
        if has_prior:
            total = total + prior[k, t, at, :]
        if last:
            here, there = means[0, max(-b, 0), t, at, :], means[a, max(b, 0), t, at, :]
            cov[k, t, at, :] = (total - here * scale * there) * scale
        else:
            maps[k, t, at, :] = total

    half = GROUP // 2
    wanted = [
        [k for k, (a, b) in enumerate(LAG_LIST) if t < tiles or b != 0]
        for t in range(ring)
    ]

    def product(i, t, slot, k):
        a, b = LAG_LIST[k]
        return value(i, t, slot, max(-b, 0)) * value(i, t, slot + a, max(b, 0))

    for t in range(ring):
        for k in wanted[t]:
            if LAG_LIST[k][0] > 0:
                first, second = [
                    over_blocks(lambda i, j=j: product(i, t, j, k)) for j in range(2)
                ]
                put_map(k, t, slice(0, GROUP), fold_two(first, second))

    def products(t, g):
        at = pl.ds(pl.multiple_of((g + 1) * GROUP, GROUP), GROUP)
        for a in range(REACH + 1):
            chosen = [k for k in wanted[t] if LAG_LIST[k][0] == a]
            folds = {k: [] for k in chosen}
            for h in range(2):
                slots = [g * GROUP + REACH + h * half + j for j in range(half)]
                totals = {k: [None] * half for k in chosen}
                for i in range(sources):
                    for k in chosen:
                        for j, slot in enumerate(slots):
                            part = product(i, t, slot, k)
                            if i > 0:
                                part = totals[k][j] + part
                            totals[k][j] = part
                for k in chosen:
                    x = merged(totals[k][0], totals[k][1], 1)
                    y = merged(totals[k][2], totals[k][3], 1)
                    folds[k].append(merged(x, y, 2))
            for k in chosen:
                put_map(k, t, at, merged(folds[k][0], folds[k][1], 4))

    def place(g):
        return pl.ds(pl.multiple_of(g * GROUP, GROUP), GROUP)

    def write(g):
        side = 2 * REACH + 1
        for k, (a, b) in enumerate(LAG_LIST):
            index = side * (a + REACH) + b + REACH
            mirror = side**2 - 1 - index
            for n, rise, offset in ((index, 0, min(b, 0)), (mirror, a, min(-b, 0))):
                row_ring = [
                    cov[k, t, place(g + 1), :] if t < tiles or offset else None
                    for t in range(ring)
                ]
                if rise > 0:
                    row_ring = [
                        row
                        if row is None
                        else pltpu.roll(
                            jnp.where(
                                sublane >= GROUP - rise, cov[k, t, place(g), :], row
                            ),
                            rise,
                            0,
                        )
                        for t, row in enumerate(row_ring)
                    ]
                for t in range(tiles):
                    lanes = slice(t * LANES, (t + 1) * LANES)
                    staged[n, place(g), lanes] = shifted(row_ring, t, offset)
                if index == mirror:
                    break

    def copy_out(g):
        rows_of = place(g)
        return pltpu.make_async_copy(
            staged.at[:, rows_of, :], out.at[:, rows_of, :], sems.at[g]
        )

    half_groups = rows // GROUP // 2
    for first in (0, half_groups):

        def sum_eight(g, carry):
            for t in range(ring):
                products(t, g)
            return carry

        lax.fori_loop(first, first + half_groups, sum_eight, 0)
        if last:

            def write_eight(g, carry):
                write(g)
                copy_out(g).start()
                return carry

            lax.fori_loop(first, first + half_groups, write_eight, 0)
    if last:

        def finish(g, carry):
            copy_out(g).wait()
            return carry

        lax.fori_loop(0, rows // GROUP, finish, 0)


def room(*parts):
    total = 0
    for leaf in jax.tree.leaves(parts):
        if hasattr(leaf, "shape") and jnp.issubdtype(leaf.dtype, jnp.floating):
            total += math.prod(leaf.shape) * jnp.dtype(leaf.dtype).itemsize
    return total * 5 // 4 + 4 * 1024 * 1024


def lag_sums(pivot, blocks, rows, tiles, frames, prior=None, last=False):
    sources = len(blocks)
    counts = [len(block) for block in blocks]
    ring = tiles + 1
    span = (rows + 2 * REACH) * GROUP
    operands = [pivot] + [a for block in blocks for a in block] + list(prior or ())
    whole = pl.BlockSpec(memory_space=pltpu.VMEM)
    map_shape = (len(LAG_LIST), ring, rows + GROUP, LANES)
    sum_shape = (ring, rows + 2 * GROUP, LANES)
    scratch = [
        pltpu.VMEM((sources, span, LANES), jnp.bfloat16),
        pltpu.VMEM((tiles, span, LANES), jnp.bfloat16),
        pltpu.VMEM((REACH + 1, sources, ring, span, LANES), jnp.float32),
    ]
    if last:
        shape = ((2 * REACH + 1) ** 2, rows, tiles * LANES)
        out_shape = jax.ShapeDtypeStruct(shape, jnp.float32)
        out_specs = pl.BlockSpec(memory_space=pl.ANY)
        scratch += [
            pltpu.VMEM(shape, jnp.float32),
            pltpu.VMEM(sum_shape, jnp.float32),
            pltpu.VMEM((REACH + 1,) * 2 + (ring, rows + GROUP, LANES), jnp.float32),
            pltpu.VMEM(map_shape, jnp.float32),
            pltpu.SemaphoreType.DMA((rows // GROUP,)),
        ]
    else:
        out_shape = (
            jax.ShapeDtypeStruct(map_shape, jnp.float32),
            jax.ShapeDtypeStruct(sum_shape, jnp.float32),
        )
        out_specs = (whole, whole)
    return pl.pallas_call(
        lambda *refs: lag_kernel(
            tiles, rows, frames, counts, prior is not None, last, *refs
        ),
        out_shape=out_shape,
        in_specs=[whole] * len(operands),
        out_specs=out_specs,
        scratch_shapes=scratch,
        compiler_params=pltpu.CompilerParams(
            vmem_limit_bytes=room(scratch, operands, out_shape)
        ),
        name="lag_maps" if last else "lag_sums",
        cost_estimate=cost(2 + 2 * sources),
    )(*operands)


def body(movie):
    frames_here, rows, width = movie.shape
    peers = lax.axis_size("frame")
    tiles = width // peers // LANES
    me = lax.axis_index("frame")
    frames = frames_here * peers
    half = peers // 2
    far = list(range(half, peers))
    near = list(range(1, half))
    strips = lax.axis_size("strip")
    up = [(i, i + 1) for i in range(strips - 1)]
    down = [(j, i) for i, j in up]
    moved = {}

    def send(k, payload, after=None):
        if after is not None:
            payload, moved[after] = lax.optimization_barrier((payload, moved[after]))
        moved[k] = lax.ppermute(payload, "frame", [(i, i ^ k) for i in range(peers)])

    ahead = pack_one(movie, me ^ far[0], peers)
    send(far[0], ahead)
    last, initial = movie[:, rows - REACH :, :], movie[:, :REACH, :]
    above = lax.ppermute(last, "strip", up)
    below = lax.ppermute(initial, "strip", down)
    packed, rest, pivot = pack_rest(movie, above, below, me, peers, far[0])
    rest, moved[far[0]] = lax.optimization_barrier((rest, moved[far[0]]))
    around = lax.ppermute(rest, "frame", [(i, i ^ far[0]) for i in range(peers)])
    for k in far[1:2] + near:
        send(k, packed[k], far[0])
    for n, k in enumerate(far[2:]):
        send(k, packed[k], far[1] if n == 0 else near[0])

    def sums(group, prior=None, last=False):
        blocks = [(moved[k], around) if k == far[0] else (moved[k],) for k in group]
        return lag_sums(pivot, blocks, rows, tiles, frames, prior, last)

    moved[0] = packed[0]
    prior = sums([0])
    prior = sums(far[:2] + near[:-1], prior)
    prior = sums(near[-1:] + far[2:-1], prior)
    return sums(far[-1:], prior, True)


def solution(mesh):
    return jax.shard_map(
        body,
        mesh=mesh,
        in_specs=(P("frame", "strip", None),),
        out_specs=P(None, "strip", "frame"),
        check_vma=False,
    )
```

```python
import math

import jax
import jax.numpy as jnp
from jax import lax
from jax.experimental import pallas as pl
from jax.experimental.pallas import tpu as pltpu
from jax.sharding import PartitionSpec as P

REACH = 2
LANES = 128
GROUP = 8
FOLD = LANES // (2 * REACH)
PAD = 2 * REACH
PAIR = 2 * GROUP
LAG_LIST = tuple(
    (a, b)
    for a in range(REACH + 1)
    for b in range(-REACH, REACH + 1)
    if a > 0 or b >= 0
)
def cost(micros):
    work = int(micros * 1e9 * 0.3)
    return pl.CostEstimate(flops=work, bytes_accessed=work // 300, transcendentals=0)


VMEM = 56 * 1024 * 1024


def shifted(ring, index, offset):
    tile = ring[index]
    if offset == 0:
        return tile
    lane = lax.broadcasted_iota(jnp.int32, tile.shape, tile.ndim - 1)
    if offset > 0:
        other = ring[(index + 1) % len(ring)]
        mixed = jnp.where(lane < offset, other, tile)
    else:
        other = ring[index - 1]
        mixed = jnp.where(lane >= LANES + offset, other, tile)
    return pltpu.roll(mixed, (-offset) % LANES, 1)


def folded_pairs(pairs):
    return -(-pairs // FOLD)


def both_rows(ref, index, row, stride):
    return jnp.concatenate(
        [ref[index, pl.ds(row + j, GROUP, stride=stride), :] for j in range(2)], axis=0
    )


def lay_out(ref, place, value, above=None, below=None):
    frames, rows, _ = value.shape
    for f in range(frames):
        start = f * (rows + PAD)
        ref[place, start + REACH : start + REACH + rows, :] = value[f].astype(jnp.float32)
        if above is not None:
            ref[place, start : start + REACH, :] = above[f].astype(jnp.float32)
            end = start + REACH + rows
            ref[place, end : end + REACH, :] = below[f].astype(jnp.float32)


def edge_sides(ref, left, right, row, stride):
    lane = lax.broadcasted_iota(jnp.int32, (PAIR, LANES), 1)
    return jnp.where(
        lane >= LANES - REACH,
        both_rows(ref, left, row, stride),
        both_rows(ref, right, row, stride),
    )


def folded_in(edge, sides, index):
    lane = lax.broadcasted_iota(jnp.int32, (PAIR, LANES), 1)
    first = 2 * REACH * index
    placed = pltpu.roll(sides, first + REACH, 1)
    return jnp.where((lane >= first) & (lane < first + 2 * REACH), placed, edge)


def write_packed(ref, places, rows, offset, outs):
    stride = rows + PAD
    pairs = outs_pairs = rows // 2 + (2 if offset == 0 else 0)
    span = pairs * PAIR
    zero = jnp.zeros((PAIR, LANES), jnp.float32)
    for part in range(folded_pairs(pairs)):

        def pair(q, edges, part=part):
            row = offset + 2 * q
            result = []
            for (own, left, right), out, edge in zip(places, outs, edges):
                for t, place in enumerate(own):
                    start = pl.multiple_of(t * span + q * PAIR, PAIR)
                    both = both_rows(ref, place, row, stride)
                    out[pl.ds(start, PAIR), :] = both.astype(jnp.bfloat16)
                sides = edge_sides(ref, left, right, row, stride)
                result.append(folded_in(edge, sides, q - part * FOLD))
            return tuple(result)

        first, last = part * FOLD, min((part + 1) * FOLD, outs_pairs)
        unroll = 8 if (last - first) % 8 == 0 else 1
        edges = lax.fori_loop(first, last, pair, (zero,) * len(outs), unroll=unroll)
        for (own, _, _), out, edge in zip(places, outs, edges):
            start = len(own) * span + part * PAIR
            out[start : start + PAIR, :] = edge.astype(jnp.bfloat16)


def pack_one_kernel(tiles, block_ref, main_ref, left_ref, right_ref, out_ref, values):
    rows = main_ref.shape[1]
    block, blocks = block_ref[0], block_ref[1]
    for t in range(tiles):
        lay_out(values, t, main_ref[:, :, t * LANES : (t + 1) * LANES])
    lay_out(values, tiles, left_ref[...])
    lay_out(values, tiles + 1, right_ref[...])

    @pl.when(block == 0)
    def _():
        values[tiles] = jnp.zeros(values.shape[1:], jnp.float32)

    @pl.when(block == blocks - 1)
    def _():
        values[tiles + 1] = jnp.zeros(values.shape[1:], jnp.float32)

    places = [(list(range(tiles)), tiles, tiles + 1)]
    write_packed(values, places, rows, REACH, [out_ref])


def packed_length(rows, tiles):
    return tiles * rows * GROUP + folded_pairs(rows // 2) * PAIR


def pack_one(movie, block, blocks):
    frames, rows, width = movie.shape
    columns = width // blocks
    tiles = columns // LANES
    last = width // LANES - 1
    length = packed_length(rows, tiles)
    return pl.pallas_call(
        lambda *refs: pack_one_kernel(tiles, *refs),
        out_shape=jax.ShapeDtypeStruct((length, LANES), jnp.bfloat16),
        grid_spec=pltpu.PrefetchScalarGridSpec(
            num_scalar_prefetch=1,
            grid=(1,),
            in_specs=[
                pl.BlockSpec((frames, rows, columns), lambda i, s: (0, 0, s[0])),
                pl.BlockSpec(
                    (frames, rows, LANES),
                    lambda i, s: (0, 0, jnp.maximum(s[0] * tiles - 1, 0)),
                ),
                pl.BlockSpec(
                    (frames, rows, LANES),
                    lambda i, s: (0, 0, jnp.minimum(s[0] * tiles + tiles, last)),
                ),
            ],
            out_specs=pl.BlockSpec((length, LANES), lambda i, s: (0, 0)),
            scratch_shapes=[
                pltpu.VMEM((tiles + 2, frames * (rows + PAD), LANES), jnp.float32)
            ],
        ),
        compiler_params=pltpu.CompilerParams(vmem_limit_bytes=VMEM),
        name="pack_one",
        cost_estimate=cost(3),
    )(jnp.stack([block, jnp.int32(blocks)]), movie, movie, movie)


def pack_kernel(tiles, skip, me_ref, movie_ref, above_ref, below_ref, *refs):
    outs, rest, pivot, values = list(refs[:-3]), refs[-3], refs[-2], refs[-1]
    frames, rows, width = movie_ref.shape
    stride = rows + PAD
    count = width // LANES
    blocks = count // tiles
    zero = jnp.zeros((frames * stride, LANES), jnp.float32)
    values[0] = zero
    values[count + 1] = zero
    for t in range(count):
        lanes = slice(t * LANES, (t + 1) * LANES)
        lay_out(
            values,
            t + 1,
            movie_ref[:, :, lanes],
            above_ref[:, :, lanes],
            below_ref[:, :, lanes],
        )
    places = []
    for k in range(blocks):
        first = 1 + (me_ref[0] ^ k) * tiles
        places.append(([first + t for t in range(tiles)], first - 1, first + tiles))
    kept = [k for k in range(blocks) if k != skip]
    write_packed(values, [places[k] for k in kept], rows, 0, outs)

    own, left, right = places[skip]
    edge = jnp.zeros((PAIR, LANES), jnp.float32)
    for n, row in enumerate((0, rows + REACH)):
        for t, place in enumerate(own):
            both = both_rows(values, place, row, stride)
            start = (t * 2 + n) * PAIR
            rest[start : start + PAIR, :] = both.astype(jnp.bfloat16)
        edge = folded_in(edge, edge_sides(values, left, right, row, stride), n)
    rest[tiles * 2 * PAIR :, :] = edge.astype(jnp.bfloat16)

    own, left, right = places[0]
    lane = lax.broadcasted_iota(jnp.int32, (PAIR, LANES), 1)

    def first_frame(place, row):
        parts = [
            jnp.broadcast_to(values[place, pl.ds(row + j, 1), :], (GROUP, LANES))
            for j in range(2)
        ]
        return jnp.concatenate(parts, axis=0)

    def pair(q, carry):
        at = pl.ds(pl.multiple_of(q * PAIR, PAIR), PAIR)
        for t, place in enumerate(own):
            pivot[t, at, :] = first_frame(place, 2 * q).astype(jnp.bfloat16)
        sides = jnp.where(
            lane >= LANES - REACH, first_frame(left, 2 * q), first_frame(right, 2 * q)
        )
        pivot[tiles, at, :] = sides.astype(jnp.bfloat16)
        return carry

    lax.fori_loop(0, rows // 2 + 2, pair, 0, unroll=2)


def pack_rest(movie, above, below, me, blocks, skip):
    frames, rows, width = movie.shape
    tiles = width // blocks // LANES
    length = tiles * (rows + 2 * REACH) * GROUP + folded_pairs(rows // 2 + 2) * PAIR
    whole = pl.BlockSpec(memory_space=pltpu.VMEM)
    kept = [k for k in range(blocks) if k != skip]
    shapes = [(length, LANES)] * len(kept)
    shapes += [((tiles * 2 + 1) * PAIR, LANES)]
    shapes += [(tiles + 1, (rows + 2 * REACH) * GROUP, LANES)]
    results = pl.pallas_call(
        lambda *refs: pack_kernel(tiles, skip, *refs),
        out_shape=[jax.ShapeDtypeStruct(shape, jnp.bfloat16) for shape in shapes],
        in_specs=[pl.BlockSpec(memory_space=pltpu.SMEM)] + [whole] * 3,
        out_specs=[whole] * len(shapes),
        scratch_shapes=[
            pltpu.VMEM((width // LANES + 2, frames * (rows + PAD), LANES), jnp.float32)
        ],
        compiler_params=pltpu.CompilerParams(vmem_limit_bytes=VMEM),
        name="pack_rest",
        cost_estimate=cost(5),
    )(me[None], movie, above, below)
    return dict(zip(kept, results)), results[-2], results[-1]


def unfolded(edge, index):
    shift = 2 * LANES - 2 * REACH * index - REACH
    return pltpu.roll(edge, lax.rem(shift, LANES), 1)


def unfold_edges(tiles, rows, block, edges, i):
    pairs = rows // 2 + 2

    def put(q, edge, index):
        start = q * PAIR
        if not isinstance(start, int):
            start = pl.multiple_of(start, PAIR)
        edges[i, pl.ds(start, PAIR), :] = unfolded(edge, index).astype(jnp.bfloat16)

    def tile_of(ref, start):
        return ref[start : start + PAIR, :].astype(jnp.float32)

    body = block[0]
    if len(block) > 1:
        around = tile_of(block[1], tiles * 2 * PAIR)
        put(0, around, 0)
        put(pairs - 1, around, 1)
        pairs, lead = rows // 2, 1
    else:
        lead = 0
    for part in range(folded_pairs(pairs)):
        edge = tile_of(body, (tiles * pairs + part) * PAIR)

        def fill(q, carry, part=part, edge=edge):
            put(q + lead, edge, q - part * FOLD)
            return carry

        first, last = part * FOLD, min((part + 1) * FOLD, pairs)
        unroll = 8 if (last - first) % 8 == 0 else 1
        lax.fori_loop(first, last, fill, 0, unroll=unroll)


def merged(first, second, distance):
    row = lax.broadcasted_iota(jnp.int32, first.shape, 0)
    low = (row & distance) == 0
    kept = jnp.where(low, first, second)
    moved = jnp.where(low, second, first)
    return kept + pltpu.roll(moved, GROUP - distance, 0)


def lag_kernel(tiles, rows, frames, counts, has_prior, last, *refs):
    refs = list(refs)
    pivot_ref = refs[0]
    refs = refs[1:]
    sources = len(counts)
    blocks = []
    for count in counts:
        blocks.append(refs[:count])
        refs = refs[count:]
    prior = None
    if has_prior:
        prior, prior_sum = refs[:2]
        refs = refs[2:]
    if last:
        out, edges, rings, shifts, staged, sums, means, cov, sems = refs
    else:
        maps, sums, edges, rings, shifts = refs
    ring = tiles + 1
    span = (rows + 2 * REACH) * GROUP

    for i, block in enumerate(blocks):
        unfold_edges(tiles, rows, block, edges, i)
        if len(block) > 1:
            body, around = block
            for t in range(tiles):
                start = t * rows * GROUP
                rings[t, PAIR : span - PAIR, :] = body[start : start + rows * GROUP, :]
                start = t * 2 * PAIR
                rings[t, :PAIR, :] = around[start : start + PAIR, :]
                rings[t, span - PAIR :, :] = around[start + PAIR : start + 2 * PAIR, :]

    def raw_values(i, t, start, size):
        if t == tiles:
            return edges[i, pl.ds(start, size), :]
        if len(blocks[i]) > 1:
            return rings[t, pl.ds(start, size), :]
        start = pl.multiple_of(t * span + start, PAIR)
        return blocks[i][0][pl.ds(start, size), :]

    source = lax.broadcasted_iota(jnp.int32, (2 * LANES, LANES), 0)
    target = lax.broadcasted_iota(jnp.int32, (2 * LANES, LANES), 1)
    moves = jnp.concatenate(
        [jnp.where(source == target + b, 1.0, 0.0) for b in range(1, REACH + 1)], axis=1
    ).astype(jnp.bfloat16)
    size = span // (2 if sources < 3 else 17)
    if size % PAIR or span % size:
        size = PAIR

    def spread(c, carry):
        start = pl.multiple_of(c * size, PAIR)
        at = pl.ds(start, size)
        raw = [[pivot_ref[t, at, :] for t in range(ring)]]
        for i in range(sources):
            raw.append([raw_values(i, t, start, size) for t in range(ring)])
        wide = jnp.concatenate(
            [
                jnp.concatenate([r[t], r[(t + 1) % ring]], axis=1)
                for r in raw
                for t in range(ring)
            ],
            axis=0,
        )
        moved = jnp.dot(wide, moves, preferred_element_type=jnp.float32)

        def version(i, t, b):
            if b == 0:
                return raw[i][t].astype(jnp.float32)
            first = (i * ring + t) * size
            return moved[first : first + size, (b - 1) * LANES : b * LANES]

        for t in range(ring):
            for b in range(REACH + 1):
                pivot = version(0, t, b)
                for i in range(1, sources + 1):
                    shifts[b, i - 1, t, at, :] = version(i, t, b) - pivot
        return carry

    lax.fori_loop(0, span // size, spread, 0)

    def value(i, t, slot, b):
        start = slot * GROUP
        if not isinstance(start, int):
            start = pl.multiple_of(start, GROUP)
        return shifts[b, i, t, pl.ds(start, GROUP), :]

    def over_blocks(term):
        total = term(0)
        for i in range(1, sources):
            total = total + term(i)
        return total

    def fold_rows(parts):
        distance = 1
        while len(parts) > 1:
            parts = [merged(x, y, distance) for x, y in zip(parts[::2], parts[1::2])]
            distance *= 2
        return parts[0]

    def fold_two(first, second):
        total = merged(first, second, 1)
        total = total + pltpu.roll(total, GROUP - 2, 0)
        return total + pltpu.roll(total, GROUP // 2, 0)

    for t in range(ring):

        def put_sum(at, total, t=t):
            if has_prior:
                total = total + prior_sum[t, at, :]
            sums[t, at, :] = total

        def row_sum(slot, t=t):
            return over_blocks(lambda i: value(i, t, slot, 0))

        put_sum(slice(0, GROUP), fold_two(row_sum(0), row_sum(1)))
        put_sum(
            slice(rows + GROUP, rows + 2 * GROUP),
            fold_two(row_sum(rows + REACH), row_sum(rows + REACH + 1)),
        )

        def sum_rows(g, carry, t=t):
            total = fold_rows([row_sum(g * GROUP + REACH + j) for j in range(GROUP)])
            put_sum(pl.ds(pl.multiple_of((g + 1) * GROUP, GROUP), GROUP), total)
            return carry

        lax.fori_loop(0, rows // GROUP, sum_rows, 0, unroll=2)

    scale = 1.0 / frames
    sublane = lax.broadcasted_iota(jnp.int32, (GROUP, LANES), 0)
    if last:

        def spread_sums(g, carry):
            at = pl.ds(pl.multiple_of(g * GROUP, GROUP), GROUP)
            after = pl.ds(pl.multiple_of((g + 1) * GROUP, GROUP), GROUP)
            for a in range(REACH + 1):
                row_ring = [sums[t, at, :] for t in range(ring)]
                if a > 0:
                    row_ring = [
                        pltpu.roll(
                            jnp.where(sublane < a, sums[t, after, :], row), GROUP - a, 0
                        )
                        for t, row in enumerate(row_ring)
                    ]
                for t in range(ring):
                    for b in range(REACH + 1):
                        means[a, b, t, at, :] = shifted(row_ring, t, b)
            return carry

        lax.fori_loop(0, rows // GROUP + 1, spread_sums, 0)

    def put_map(k, t, at, total):
        a, b = LAG_LIST[k]
        if has_prior:
            total = total + prior[k, t, at, :]
        if last:
            here, there = means[0, max(-b, 0), t, at, :], means[a, max(b, 0), t, at, :]
            cov[k, t, at, :] = (total - here * scale * there) * scale
        else:
            maps[k, t, at, :] = total

    half = GROUP // 2
    wanted = [
        [k for k, (a, b) in enumerate(LAG_LIST) if t < tiles or b != 0]
        for t in range(ring)
    ]

    def product(i, t, slot, k):
        a, b = LAG_LIST[k]
        return value(i, t, slot, max(-b, 0)) * value(i, t, slot + a, max(b, 0))

    for t in range(ring):
        for k in wanted[t]:
            if LAG_LIST[k][0] > 0:
                first, second = [
                    over_blocks(lambda i, j=j: product(i, t, j, k)) for j in range(2)
                ]
                put_map(k, t, slice(0, GROUP), fold_two(first, second))

    def products(t, g):
        at = pl.ds(pl.multiple_of((g + 1) * GROUP, GROUP), GROUP)
        for a in range(REACH + 1):
            chosen = [k for k in wanted[t] if LAG_LIST[k][0] == a]
            folds = {k: [] for k in chosen}
            for h in range(2):
                slots = [g * GROUP + REACH + h * half + j for j in range(half)]
                totals = {k: [None] * half for k in chosen}
                for i in range(sources):
                    for k in chosen:
                        for j, slot in enumerate(slots):
                            part = product(i, t, slot, k)
                            if i > 0:
                                part = totals[k][j] + part
                            totals[k][j] = part
                for k in chosen:
                    x = merged(totals[k][0], totals[k][1], 1)
                    y = merged(totals[k][2], totals[k][3], 1)
                    folds[k].append(merged(x, y, 2))
            for k in chosen:
                put_map(k, t, at, merged(folds[k][0], folds[k][1], 4))

    def place(g):
        return pl.ds(pl.multiple_of(g * GROUP, GROUP), GROUP)

    def write(g):
        side = 2 * REACH + 1
        for k, (a, b) in enumerate(LAG_LIST):
            index = side * (a + REACH) + b + REACH
            mirror = side**2 - 1 - index
            for n, rise, offset in ((index, 0, min(b, 0)), (mirror, a, min(-b, 0))):
                row_ring = [
                    cov[k, t, place(g + 1), :] if t < tiles or offset else None
                    for t in range(ring)
                ]
                if rise > 0:
                    row_ring = [
                        row
                        if row is None
                        else pltpu.roll(
                            jnp.where(
                                sublane >= GROUP - rise, cov[k, t, place(g), :], row
                            ),
                            rise,
                            0,
                        )
                        for t, row in enumerate(row_ring)
                    ]
                for t in range(tiles):
                    lanes = slice(t * LANES, (t + 1) * LANES)
                    staged[n, place(g), lanes] = shifted(row_ring, t, offset)
                if index == mirror:
                    break

    def copy_out(g):
        rows_of = place(g)
        return pltpu.make_async_copy(
            staged.at[:, rows_of, :], out.at[:, rows_of, :], sems.at[g]
        )

    half_groups = rows // GROUP // 2
    for first in (0, half_groups):

        def sum_eight(g, carry):
            for t in range(ring):
                products(t, g)
            return carry

        lax.fori_loop(first, first + half_groups, sum_eight, 0)
        if last:

            def write_eight(g, carry):
                write(g)
                copy_out(g).start()
                return carry

            lax.fori_loop(first, first + half_groups, write_eight, 0)
    if last:

        def finish(g, carry):
            copy_out(g).wait()
            return carry

        lax.fori_loop(0, rows // GROUP, finish, 0)


def room(*parts):
    total = 0
    for leaf in jax.tree.leaves(parts):
        if hasattr(leaf, "shape") and jnp.issubdtype(leaf.dtype, jnp.floating):
            total += math.prod(leaf.shape) * jnp.dtype(leaf.dtype).itemsize
    return total * 5 // 4 + 4 * 1024 * 1024


def lag_sums(pivot, blocks, rows, tiles, frames, prior=None, last=False):
    sources = len(blocks)
    counts = [len(block) for block in blocks]
    ring = tiles + 1
    span = (rows + 2 * REACH) * GROUP
    operands = [pivot] + [a for block in blocks for a in block] + list(prior or ())
    whole = pl.BlockSpec(memory_space=pltpu.VMEM)
    map_shape = (len(LAG_LIST), ring, rows + GROUP, LANES)
    sum_shape = (ring, rows + 2 * GROUP, LANES)
    scratch = [
        pltpu.VMEM((sources, span, LANES), jnp.bfloat16),
        pltpu.VMEM((tiles, span, LANES), jnp.bfloat16),
        pltpu.VMEM((REACH + 1, sources, ring, span, LANES), jnp.float32),
    ]
    if last:
        shape = ((2 * REACH + 1) ** 2, rows, tiles * LANES)
        out_shape = jax.ShapeDtypeStruct(shape, jnp.float32)
        out_specs = pl.BlockSpec(memory_space=pl.ANY)
        scratch += [
            pltpu.VMEM(shape, jnp.float32),
            pltpu.VMEM(sum_shape, jnp.float32),
            pltpu.VMEM((REACH + 1,) * 2 + (ring, rows + GROUP, LANES), jnp.float32),
            pltpu.VMEM(map_shape, jnp.float32),
            pltpu.SemaphoreType.DMA((rows // GROUP,)),
        ]
    else:
        out_shape = (
            jax.ShapeDtypeStruct(map_shape, jnp.float32),
            jax.ShapeDtypeStruct(sum_shape, jnp.float32),
        )
        out_specs = (whole, whole)
    return pl.pallas_call(
        lambda *refs: lag_kernel(
            tiles, rows, frames, counts, prior is not None, last, *refs
        ),
        out_shape=out_shape,
        in_specs=[whole] * len(operands),
        out_specs=out_specs,
        scratch_shapes=scratch,
        compiler_params=pltpu.CompilerParams(
            vmem_limit_bytes=room(scratch, operands, out_shape)
        ),
        name="lag_maps" if last else "lag_sums",
        cost_estimate=cost(2 + 2 * sources),
    )(*operands)


def body(movie):
    frames_here, rows, width = movie.shape
    peers = lax.axis_size("frame")
    tiles = width // peers // LANES
    me = lax.axis_index("frame")
    frames = frames_here * peers
    half = peers // 2
    far = list(range(half, peers))
    near = list(range(1, half))
    strips = lax.axis_size("strip")
    up = [(i, i + 1) for i in range(strips - 1)]
    down = [(j, i) for i, j in up]
    moved = {}

    def send(k, payload, after=None):
        if after is not None:
            payload, moved[after] = lax.optimization_barrier((payload, moved[after]))
        moved[k] = lax.ppermute(payload, "frame", [(i, i ^ k) for i in range(peers)])

    ahead = pack_one(movie, me ^ far[0], peers)
    send(far[0], ahead)
    last, initial = movie[:, rows - REACH :, :], movie[:, :REACH, :]
    above = lax.ppermute(last, "strip", up)
    below = lax.ppermute(initial, "strip", down)
    packed, rest, pivot = pack_rest(movie, above, below, me, peers, far[0])
    rest, moved[far[0]] = lax.optimization_barrier((rest, moved[far[0]]))
    around = lax.ppermute(rest, "frame", [(i, i ^ far[0]) for i in range(peers)])
    for k in far[1:2] + near:
        send(k, packed[k], far[0])
    for n, k in enumerate(far[2:]):
        send(k, packed[k], far[1] if n == 0 else near[0])

    def sums(group, prior=None, last=False):
        blocks = [(moved[k], around) if k == far[0] else (moved[k],) for k in group]
        return lag_sums(pivot, blocks, rows, tiles, frames, prior, last)

    moved[0] = packed[0]
    prior = sums([0])
    prior = sums(far[:2] + near[:-1], prior)
    prior = sums(near[-1:] + far[2:-1], prior)
    return sums(far[-1:], prior, True)


def solution(mesh):
    return jax.shard_map(
        body,
        mesh=mesh,
        in_specs=(P("frame", "strip", None),),
        out_specs=P(None, "strip", "frame"),
        check_vma=False,
    )
```
